128 devices in a mesh: row: 16 (over z, x_lo, core), col: 8 (over x_hi, y).
Axes of the slice: x: 4 (x_hi: 2, x_lo: 2; x = x_hi * 2 + x_lo), y: 4, z: 4, core: 2. Of those that a mesh axis runs over, the one named last changes fastest.
Arguments:
- pair: bfloat16 [512, 512, 128], P('row', 'col'), may hold values from -30 to 30
- in_gain: float32 [2, 128], replicated, may hold values from 0.5 to 1.5
- proj_weight: bfloat16 [2, 128, 512], replicated, may hold values from -0.5 to 0.5
- gate_weight: bfloat16 [2, 128, 128], replicated, may hold values from -0.5 to 0.5
- out_gain: float32 [2, 128], replicated, may hold values from 0.5 to 1.5
- out_weight: bfloat16 [2, 128, 128], replicated, may hold values from -0.5 to 0.5
Outputs:
- after_outgoing: bfloat16 [512, 512, 128], P('row', 'col')
- after_incoming: bfloat16 [512, 512, 128], P('row', 'col')
The draws below stay inside these ranges and needn't reach their ends.
All inputs are finite; a program needn't handle non-finite values.
Results may differ from the reference program's by a relative error of at most 0.007.
Values may be sent and summed in bfloat16 or wider, within the bound.
A program may use at most 64 MiB of HBM per device.

```python
import jax
import jax.numpy as jnp
from jax import lax

C = 128
H = 128
N = 512
ROWS = 32


def draw_pair(key, part):
    key = jax.random.fold_in(key, 11)
    keys = jax.random.split(key, 3)
    cell_scale = jnp.exp(jax.random.uniform(keys[0], (N, N, 1), jnp.float32, -1.0, 1.0))
    chan_scale = jnp.exp(jax.random.uniform(keys[1], (1, 1, C), jnp.float32, -1.0, 1.0))
    base = jnp.clip(jax.random.normal(keys[2], (N, N, C), jnp.float32), -4.0, 4.0)
    values = base * cell_scale * chan_scale
    return values.astype(jnp.bfloat16)


def bell_draw(stream_key, shape, deviation, reach, kind=jnp.bfloat16):
    return jnp.clip(deviation * jax.random.normal(stream_key, shape, jnp.float32), -reach, reach).astype(kind)


def setup_inputs(seed: int = 0) -> dict:
    streams_of = jax.random.split(jax.random.key(seed), 7)
    pair = draw_pair(jax.random.fold_in(streams_of[6], 71), 0)
    in_gain = jnp.clip(1.0 + 0.1 * jax.random.normal(streams_of[1], (2, C), jnp.float32), 0.5, 1.5)
    proj_weight = bell_draw(streams_of[2], (2, C, 4 * H), C ** -0.5, 0.5)
    gate_weight = bell_draw(streams_of[3], (2, C, C), C ** -0.5, 0.5)
    out_gain = jnp.clip(1.0 + 0.1 * jax.random.normal(streams_of[4], (2, H), jnp.float32), 0.5, 1.5)
    out_weight = bell_draw(streams_of[5], (2, H, C), H ** -0.5, 0.5)
    return {"pair": pair, "in_gain": in_gain, "proj_weight": proj_weight, "gate_weight": gate_weight, "out_gain": out_gain, "out_weight": out_weight}


EPS = 1e-05

def layer_norm(values, gain):
    values = values.astype(jnp.float32)
    average = lax.optimization_barrier(jnp.mean(values, axis=-1, keepdims=True))
    centered = values - average
    variance = lax.optimization_barrier(jnp.mean(centered * centered, axis=-1, keepdims=True))
    return centered * lax.rsqrt(variance + EPS) * gain.astype(jnp.float32)

def halves(z_block, which, in_gain, proj_weight):
    normed = layer_norm(z_block, in_gain[which]).astype(jnp.bfloat16)
    projected = jnp.dot(normed.astype(jnp.float32), proj_weight[which].astype(jnp.float32))
    left_side = (jax.nn.sigmoid(projected[..., 0:H]) * projected[..., H:2 * H]).astype(jnp.bfloat16)
    right_side = (jax.nn.sigmoid(projected[..., 2 * H:3 * H]) * projected[..., 3 * H:4 * H]).astype(jnp.bfloat16)
    return (left_side, right_side)

def one_update(z_field, which, in_gain, proj_weight, gate_weight, out_gain, out_weight):
    z_blocks = z_field.reshape(N // ROWS, ROWS, N, C)
    left_side, right_side = lax.map(lambda block_rows: halves(block_rows, which, in_gain, proj_weight), z_blocks)
    left_chan = jnp.moveaxis(left_side.reshape(N, N, H), 2, 0)
    right_chan = jnp.moveaxis(right_side.reshape(N, N, H), 2, 0)

    def channel(operands):
        first_op = operands[0].astype(jnp.float32)
        second_op = operands[1].astype(jnp.float32)
        if which == 0:
            product = jnp.dot(first_op, second_op.T)
        else:
            product = jnp.dot(first_op.T, second_op)
        return product.astype(jnp.bfloat16)
    triangle = jnp.moveaxis(lax.map(channel, (left_chan, right_chan)), 0, 2)

    def finish(inputs):
        z_block, tri_block = inputs
        normed = layer_norm(z_block, in_gain[which]).astype(jnp.bfloat16)
        tnorm = layer_norm(tri_block, out_gain[which]).astype(jnp.bfloat16)
        gating = jax.nn.sigmoid(jnp.dot(normed.astype(jnp.float32), gate_weight[which].astype(jnp.float32)))
        change = gating * jnp.dot(tnorm.astype(jnp.float32), out_weight[which].astype(jnp.float32))
        return (z_block.astype(jnp.float32) + change).astype(jnp.bfloat16)
    result = lax.map(finish, (z_blocks, triangle.reshape(N // ROWS, ROWS, N, H)))
    return result.reshape(N, N, C)

def reference(pair, in_gain, proj_weight, gate_weight, out_gain, out_weight):
    after_outgoing = one_update(pair, 0, in_gain, proj_weight, gate_weight, out_gain, out_weight)
    after_incoming = one_update(after_outgoing, 1, in_gain, proj_weight, gate_weight, out_gain, out_weight)
    return (after_outgoing, after_incoming)
```

```python
import jax
import jax.numpy as jnp
from jax import lax
from jax.experimental import pallas as pl
from jax.experimental.pallas import tpu as pltpu
from jax.sharding import PartitionSpec as P

EPS = 1e-05
MESH = pl.DeviceIdType.MESH
F32 = jnp.float32
BF16 = jnp.bfloat16
NT = (((1,), (1,)), ((), ()))
TN = (((0,), (0,)), ((), ()))


def norm_rows(values, gain):
    centered = values - jnp.mean(values, axis=0, keepdims=True)
    variance = jnp.mean(centered * centered, axis=0, keepdims=True)
    return (centered * lax.rsqrt(variance + EPS) * gain).astype(BF16)


def sigmoid(values):
    return 0.5 * jnp.tanh(0.5 * values) + 0.5


def swap_halves(first, second):
    return (
        jnp.concatenate([first[:, :64], second[:, :64]], axis=1),
        jnp.concatenate([first[:, 64:], second[:, 64:]], axis=1),
    )


def kernel(
    pair,
    in_gain,
    proj_weight,
    gate_weight,
    out_gain,
    out_weight,
    out0,
    out1,
    eye,
    proj_t,
    gate_t,
    outw_t,
    gains,
    zt,
    normed,
    flat_l,
    flat_r,
    send,
    recv,
    left,
    right,
    tsend,
    trecv,
    send_sem,
    recv_sem,
    tsend_sem,
    trecv_sem,
):
    row, col = lax.axis_index("row"), lax.axis_index("col")
    mine = row * 8 + col

    def peer(step):
        dr, dc = step // 8, lax.rem(step, 8)
        z = lax.rem(row // 4 + dr // 4, 4)
        lo = jnp.bitwise_xor(lax.rem(row, 4), lax.rem(dr, 4))
        hi = jnp.bitwise_xor(col // 4, dc // 4)
        y = lax.rem(lax.rem(col, 4) + lax.rem(dc, 4), 4)
        return z * 4 + lo, hi * 4 + y

    barrier = pltpu.get_barrier_semaphore()

    def greet(step, carry):
        pl.semaphore_signal(barrier, inc=1, device_id=peer(step), device_id_type=MESH)
        return carry

    lax.fori_loop(1, 128, greet, 0, unroll=8)

    ident = (
        lax.broadcasted_iota(jnp.int32, (128, 128), 0)
        == lax.broadcasted_iota(jnp.int32, (128, 128), 1)
    ).astype(F32)
    eye[...] = ident.astype(BF16)

    def flip(block):
        return lax.dot_general(eye[...], block, NT, preferred_element_type=F32)

    for u in range(2):
        for b in range(4):
            proj_t[u, 128 * b : 128 * (b + 1), :] = flip(
                proj_weight[u, :, 128 * b : 128 * (b + 1)]
            ).astype(BF16)
        gate_t[u] = flip(gate_weight[u]).astype(BF16)
        outw_t[u] = flip(out_weight[u]).astype(BF16)
        gains[0, u] = jnp.transpose(jnp.broadcast_to(in_gain[u : u + 1, :], (128, 128)))
        gains[1, u] = jnp.transpose(jnp.broadcast_to(out_gain[u : u + 1, :], (128, 128)))

    def project(u, q, zq):
        zt[q] = zq
        nq = norm_rows(zq, gains[0, u])
        normed[q] = nq
        proj = jnp.dot(proj_t[u], nq, preferred_element_type=F32)
        flat_l[pl.ds(q, 128, stride=16), :] = sigmoid(proj[0:128]) * proj[128:256]
        flat_r[pl.ds(q, 128, stride=16), :] = sigmoid(proj[256:384]) * proj[384:512]

    def first(q, carry):
        block = jnp.concatenate([pair[q], pair[q + 16]], axis=0)
        project(0, q, flip(block))
        return carry

    lax.fori_loop(0, 16, first, 0)
    pl.semaphore_wait(barrier, 127)

    for u in range(2):

        def pack(d):
            rows = pl.ds(pl.multiple_of(d * 16, 16), 16)
            send[u, d, 0] = flat_l[rows, :].astype(BF16)
            send[u, d, 1] = flat_r[rows, :].astype(BF16)

        def out_lr(step, carry):
            tr, tc = peer(step)
            d = tr * 8 + tc
            pack(d)
            pltpu.make_async_remote_copy(
                src_ref=send.at[u, d],
                dst_ref=recv.at[u, mine],
                send_sem=send_sem.at[u],
                recv_sem=recv_sem.at[u],
                device_id=(tr, tc),
                device_id_type=MESH,
            ).start()
            return carry

        lax.fori_loop(1, 128, out_lr, 0, unroll=2)
        pack(mine)
        recv[u, mine] = send[u, mine]
        pltpu.make_async_copy(
            recv.at[u, pl.ds(0, 127)], recv.at[u, pl.ds(0, 127)], recv_sem.at[u]
        ).wait()

        def arrange(r, carry):
            at = pl.multiple_of(r * 32, 32)
            for side, whole in enumerate((left, right)):
                for m in range(4):
                    lo, hi = swap_halves(recv[u, r * 8 + 2 * m, side], recv[u, r * 8 + 2 * m + 1, side])
                    whole[pl.ds(at, 16), 128 * m : 128 * (m + 1)] = lo
                    whole[pl.ds(at + 16, 16), 128 * m : 128 * (m + 1)] = hi
            return carry

        lax.fori_loop(0, 16, arrange, 0)

        for b in range(4):
            if u == 0:
                tri = lax.dot_general(
                    left[128 * b : 128 * (b + 1), :], right[...], NT, preferred_element_type=F32
                ).astype(BF16)
            else:
                tri = lax.dot_general(
                    left[:, 128 * b : 128 * (b + 1)], right[...], TN, preferred_element_type=F32
                ).astype(BF16)
            for rr in range(4):
                for m in range(4):
                    lo, hi = swap_halves(
                        tri[32 * rr : 32 * rr + 16, 128 * m : 128 * (m + 1)],
                        tri[32 * rr + 16 : 32 * rr + 32, 128 * m : 128 * (m + 1)],
                    )
                    tsend[u, (4 * b + rr) * 8 + 2 * m] = lo
                    tsend[u, (4 * b + rr) * 8 + 2 * m + 1] = hi

        def out_t(step, carry):
            tr, tc = peer(step)
            pltpu.make_async_remote_copy(
                src_ref=tsend.at[u, tr * 8 + tc],
                dst_ref=trecv.at[u, mine],
                send_sem=tsend_sem.at[u],
                recv_sem=trecv_sem.at[u],
                device_id=(tr, tc),
                device_id_type=MESH,
            ).start()
            return carry

        lax.fori_loop(1, 128, out_t, 0, unroll=8)
        trecv[u, mine] = tsend[u, mine]
        pltpu.make_async_copy(
            trecv.at[u, pl.ds(0, 127)], trecv.at[u, pl.ds(0, 127)], trecv_sem.at[u]
        ).wait()

        def widen(h, carry):
            flat_l[pl.ds(pl.multiple_of(h * 64, 64), 64), :] = (
                trecv[u, pl.ds(h * 4, 4)].astype(F32).reshape(64, 128)
            )
            return carry

        lax.fori_loop(0, 32, widen, 0, unroll=4)

        def finish(q, carry):
            tn = norm_rows(flat_l[pl.ds(q, 128, stride=16), :], gains[1, u])
            gate = sigmoid(jnp.dot(gate_t[u], normed[q], preferred_element_type=F32))
            change = gate * jnp.dot(outw_t[u], tn, preferred_element_type=F32)
            new = (zt[q] + change).astype(BF16)
            flipped = flip(new).astype(BF16)
            target = (out0, out1)[u]
            target[q] = flipped[:64]
            target[q + 16] = flipped[64:]
            zt[q] = new.astype(F32)
            return carry

        lax.fori_loop(0, 16, finish, 0)
        if u == 0:

            def again(q, carry):
                project(1, q, zt[q])
                return carry

            lax.fori_loop(0, 16, again, 0)

    for u in range(2):
        pltpu.make_async_copy(
            send.at[u, pl.ds(0, 127)], send.at[u, pl.ds(0, 127)], send_sem.at[u]
        ).wait()
        pltpu.make_async_copy(
            tsend.at[u, pl.ds(0, 127)], tsend.at[u, pl.ds(0, 127)], tsend_sem.at[u]
        ).wait()


def local(pair, in_gain, proj_weight, gate_weight, out_gain, out_weight):
    vmem = pl.BlockSpec(memory_space=pltpu.VMEM)
    shape = jax.ShapeDtypeStruct(pair.shape, BF16)
    return pl.pallas_call(
        kernel,
        out_shape=(shape, shape),
        in_specs=[vmem] * 6,
        out_specs=(vmem, vmem),
        scratch_shapes=[
            pltpu.VMEM((128, 128), BF16),
            pltpu.VMEM((2, 512, 128), BF16),
            pltpu.VMEM((2, 128, 128), BF16),
            pltpu.VMEM((2, 128, 128), BF16),
            pltpu.VMEM((2, 2, 128, 128), F32),
            pltpu.VMEM((16, 128, 128), F32),
            pltpu.VMEM((16, 128, 128), BF16),
            pltpu.VMEM((2048, 128), F32),
            pltpu.VMEM((2048, 128), F32),
            pltpu.VMEM((2, 128, 2, 16, 128), BF16),
            pltpu.VMEM((2, 128, 2, 16, 128), BF16),
            pltpu.VMEM((512, 512), BF16),
            pltpu.VMEM((512, 512), BF16),
            pltpu.VMEM((2, 128, 16, 128), BF16),
            pltpu.VMEM((2, 128, 16, 128), BF16),
            pltpu.SemaphoreType.DMA((2,)),
            pltpu.SemaphoreType.DMA((2,)),
            pltpu.SemaphoreType.DMA((2,)),
            pltpu.SemaphoreType.DMA((2,)),
        ],
        compiler_params=pltpu.CompilerParams(
            collective_id=0, has_side_effects=True, vmem_limit_bytes=40 << 20
        ),
        name="triangle",
    )(pair, in_gain, proj_weight, gate_weight, out_gain, out_weight)


def solution(mesh):
    in_specs = (P("row", "col", None), P(), P(), P(), P(), P())
    out_specs = (P("row", "col", None), P("row", "col", None))
    return jax.shard_map(local, mesh=mesh, in_specs=in_specs, out_specs=out_specs, check_vma=False)
```

```python
import jax
import jax.numpy as jnp
from jax import lax
from jax.experimental import pallas as pl
from jax.experimental.pallas import tpu as pltpu
from jax.sharding import PartitionSpec as P

EPS = 1e-05
MESH = pl.DeviceIdType.MESH
F32 = jnp.float32
BF16 = jnp.bfloat16
TN = (((0,), (0,)), ((), ()))


def norm_rows(values, gain):
    centered = values - jnp.mean(values, axis=0, keepdims=True)
    variance = jnp.mean(centered * centered, axis=0, keepdims=True)
    return (centered * lax.rsqrt(variance + EPS) * gain).astype(BF16)


def sigmoid(values):
    return 0.5 * jnp.tanh(0.5 * values) + 0.5


def swap_halves(first, second):
    return (
        jnp.concatenate([first[:, :64], second[:, :64]], axis=1),
        jnp.concatenate([first[:, 64:], second[:, 64:]], axis=1),
    )


def kernel(
    pair_hbm,
    in_gain_hbm,
    proj_hbm,
    gate_hbm,
    out_gain_hbm,
    outw_hbm,
    out0,
    out1,
    pair,
    proj_w,
    gate_w,
    outw_w,
    in_gain,
    out_gain,
    proj_t,
    gate_t,
    outw_t,
    gains,
    zt,
    normed,
    flat_l,
    flat_r,
    flat_t,
    send_l,
    send_r,
    recv_l,
    recv_r,
    block0,
    block1,
    right,
    right_t,
    tsend,
    trecv,
    load_sem,
    send_sem,
    recv_r_sem,
    recv_l_sem,
    recv_t_sem,
):
    row, col = lax.axis_index("row"), lax.axis_index("col")
    mine = row * 8 + col
    outs = (out0, out1)

    def peer(step):
        dr, dc = step // 8, lax.rem(step, 8)
        z = lax.rem(row // 4 + dr // 4, 4)
        lo = jnp.bitwise_xor(lax.rem(row, 4), lax.rem(dr, 4))
        hi = jnp.bitwise_xor(col // 4, dc // 4)
        y = lax.rem(lax.rem(col, 4) + lax.rem(dc, 4), 4)
        return z * 4 + lo, hi * 4 + y

    def peer_of_pair(step):
        g, t = step // 32, lax.rem(step, 32)
        dr, parity = t // 2, lax.rem(t, 2)
        z = lax.rem(row // 4 + dr // 4, 4)
        lo = jnp.bitwise_xor(lax.rem(row, 4), lax.rem(dr, 4))
        return z * 4 + lo, jnp.bitwise_xor(col, 2 * g + parity)

    barrier = pltpu.get_barrier_semaphore()

    def greet(step, carry):
        pl.semaphore_signal(barrier, inc=1, device_id=peer(step), device_id_type=MESH)
        return carry

    lax.fori_loop(1, 128, greet, 0, unroll=8)

    loads = [
        pltpu.make_async_copy(src, dst, load_sem.at[i])
        for i, (src, dst) in enumerate(
            (
                (pair_hbm, pair),
                (proj_hbm, proj_w),
                (gate_hbm, gate_w),
                (outw_hbm, outw_w),
                (in_gain_hbm, in_gain),
                (out_gain_hbm, out_gain),
            )
        )
    ]
    for load in loads:
        load.start()
    for load in loads[1:]:
        load.wait()
    for u in range(2):
        for i, gain in enumerate((in_gain, out_gain)):
            flipped = jnp.transpose(jnp.broadcast_to(gain[u : u + 1, :], (128, 128)))
            gains[i, u] = jnp.concatenate([flipped, flipped], axis=1)
        proj_t[u] = jnp.transpose(proj_w[u])
        gate_t[u] = jnp.transpose(gate_w[u])
        outw_t[u] = jnp.transpose(outw_w[u])
    loads[0].wait()

    def project(u, q, side, flat):
        proj = jnp.dot(
            proj_t[u, 256 * side : 256 * side + 256, :], normed[q], preferred_element_type=F32
        )
        gated = sigmoid(proj[:128]) * proj[128:]
        for k in range(2):
            flat[pl.ds(2 * q + k, 128, stride=16), :] = gated[:, 128 * k : 128 * (k + 1)]

    def first(q, carry):
        block = jnp.concatenate(
            [pair[2 * q], pair[2 * q + 16], pair[2 * q + 1], pair[2 * q + 17]], axis=0
        )
        zq = jnp.transpose(block).astype(F32)
        zt[q] = zq
        normed[q] = norm_rows(zq, gains[0, 0])
        project(0, q, 1, flat_r)
        project(0, q, 0, flat_l)
        return carry

    lax.fori_loop(0, 8, first, 0, unroll=4)
    pl.semaphore_wait(barrier, 127)

    def send_side(u, flat, send, recv, sem_of, lo, hi, to):
        def one(step, carry):
            tr, tc = to(step)
            d = tr * 8 + tc
            send[u, d] = flat[pl.ds(pl.multiple_of(d * 16, 16), 16), :].astype(BF16)
            pltpu.make_async_remote_copy(
                src_ref=send.at[u, d],
                dst_ref=recv.at[u, mine],
                send_sem=send_sem.at[u],
                recv_sem=sem_of,
                device_id=(tr, tc),
                device_id_type=MESH,
            ).start()
            return carry

        lax.fori_loop(lo, hi, one, 0, unroll=4)

    def wait_tiles(ref, sem, count):
        pltpu.make_async_copy(ref.at[pl.ds(0, count)], ref.at[pl.ds(0, count)], sem).wait()

    def own(u, flat, recv):
        recv[u, mine] = flat[pl.ds(pl.multiple_of(mine * 16, 16), 16), :].astype(BF16)

    for u in range(2):
        to_left = peer if u == 0 else peer_of_pair
        send_side(u, flat_r, send_r, recv_r, recv_r_sem.at[u], 1, 128, peer)
        own(u, flat_r, recv_r)
        if u == 1:

            def late_left(q, carry):
                project(1, q, 0, flat_l)
                return carry

            lax.fori_loop(0, 8, late_left, 0, unroll=4)
        for g in range(4):
            send_side(
                u, flat_l, send_l, recv_l, recv_l_sem.at[u, g], max(32 * g, 1), 32 * g + 32, to_left
            )
        own(u, flat_l, recv_l)
        if u == 1:

            def write_first(q, carry):
                flipped = jnp.transpose(zt[q].astype(BF16))
                for k in range(2):
                    out0[2 * q + k] = flipped[128 * k : 128 * k + 64]
                    out0[2 * q + k + 16] = flipped[128 * k + 64 : 128 * k + 128]
                return carry

            lax.fori_loop(0, 8, write_first, 0, unroll=2)

        wait_tiles(recv_r.at[u], recv_r_sem.at[u], 127)

        def arrange(r, carry):
            at = pl.multiple_of(r * 32, 32)
            for m in range(4):
                lo, hi = swap_halves(recv_r[u, r * 8 + 2 * m], recv_r[u, r * 8 + 2 * m + 1])
                right[pl.ds(at, 16), 128 * m : 128 * (m + 1)] = lo
                right[pl.ds(at + 16, 16), 128 * m : 128 * (m + 1)] = hi
            return carry

        lax.fori_loop(0, 16, arrange, 0, unroll=4)
        if u == 0:
            right_t[...] = jnp.transpose(right[...])

        for g in range(4):
            wait_tiles(recv_l.at[u], recv_l_sem.at[u, g], 31 if g == 0 else 32)
            if u == 0:
                part = lax.rem(row // 4 + (4 - g), 4)
                for rr in range(4):
                    for m in range(4):
                        at = (part * 4 + rr) * 8 + 2 * m
                        lo, hi = swap_halves(recv_l[u, at], recv_l[u, at + 1])
                        block0[32 * rr : 32 * rr + 16, 128 * m : 128 * (m + 1)] = lo
                        block0[32 * rr + 16 : 32 * rr + 32, 128 * m : 128 * (m + 1)] = hi
                tri = jnp.dot(block0[...], right_t[...], preferred_element_type=F32).astype(BF16)
            else:
                part = jnp.bitwise_xor(col // 2, g)
                for r in range(16):
                    at = r * 8 + 2 * part
                    lo, hi = swap_halves(recv_l[u, at], recv_l[u, at + 1])
                    block1[32 * r : 32 * r + 16, :] = lo
                    block1[32 * r + 16 : 32 * r + 32, :] = hi
                tri = lax.dot_general(
                    block1[...], right[...], TN, preferred_element_type=F32
                ).astype(BF16)
            for rr in range(4):
                for m in range(4):
                    lo, hi = swap_halves(
                        tri[32 * rr : 32 * rr + 16, 128 * m : 128 * (m + 1)],
                        tri[32 * rr + 16 : 32 * rr + 32, 128 * m : 128 * (m + 1)],
                    )
                    tsend[u, (part * 4 + rr) * 8 + 2 * m] = lo
                    tsend[u, (part * 4 + rr) * 8 + 2 * m + 1] = hi

            def home(t, carry):
                tr = part * 4 + jnp.bitwise_xor(lax.rem(row, 4), t // 8)
                tc = jnp.bitwise_xor(col, lax.rem(t, 8))

                @pl.when(jnp.logical_or(tr != row, tc != col))
                def _():
                    pltpu.make_async_remote_copy(
                        src_ref=tsend.at[u, tr * 8 + tc],
                        dst_ref=trecv.at[u, mine],
                        send_sem=send_sem.at[u],
                        recv_sem=recv_t_sem.at[u],
                        device_id=(tr, tc),
                        device_id_type=MESH,
                    ).start()

                return carry

            lax.fori_loop(0, 32, home, 0, unroll=4)
        trecv[u, mine] = tsend[u, mine]
        wait_tiles(trecv.at[u], recv_t_sem.at[u], 127)

        def widen(h, carry):
            flat_t[pl.ds(pl.multiple_of(h * 64, 64), 64), :] = (
                trecv[u, pl.ds(h * 4, 4)].astype(F32).reshape(64, 128)
            )
            return carry

        lax.fori_loop(0, 32, widen, 0, unroll=4)

        def finish(q, carry):
            tri_q = jnp.concatenate(
                [flat_t[pl.ds(2 * q + k, 128, stride=16), :] for k in range(2)], axis=1
            )
            tn = norm_rows(tri_q, gains[1, u])
            gate = sigmoid(jnp.dot(gate_t[u], normed[q], preferred_element_type=F32))
            change = gate * jnp.dot(outw_t[u], tn, preferred_element_type=F32)
            new = (zt[q] + change).astype(BF16)
            if u == 0:
                zq = new.astype(F32)
                zt[q] = zq
                normed[q] = norm_rows(zq, gains[0, 1])
                project(1, q, 1, flat_r)
            else:
                flipped = jnp.transpose(new)
                for k in range(2):
                    out1[2 * q + k] = flipped[128 * k : 128 * k + 64]
                    out1[2 * q + k + 16] = flipped[128 * k + 64 : 128 * k + 128]
            return carry

        lax.fori_loop(0, 8, finish, 0, unroll=4)

    for u in range(2):
        for _ in range(3):
            wait_tiles(send_r.at[u], send_sem.at[u], 127)


def local(pair, in_gain, proj_weight, gate_weight, out_gain, out_weight):
    vmem = pl.BlockSpec(memory_space=pltpu.VMEM)
    hbm = pl.BlockSpec(memory_space=pltpu.HBM)
    shape = jax.ShapeDtypeStruct(pair.shape, BF16)
    tiles = pltpu.VMEM((2, 128, 16, 128), BF16)
    dma = pltpu.SemaphoreType.DMA
    return pl.pallas_call(
        kernel,
        out_shape=(shape, shape),
        in_specs=[hbm] * 6,
        out_specs=(vmem, vmem),
        scratch_shapes=[
            pltpu.VMEM((32, 64, 128), BF16),
            pltpu.VMEM((2, 128, 512), BF16),
            pltpu.VMEM((2, 128, 128), BF16),
            pltpu.VMEM((2, 128, 128), BF16),
            pltpu.VMEM((2, 128), F32),
            pltpu.VMEM((2, 128), F32),
            pltpu.VMEM((2, 512, 128), BF16),
            pltpu.VMEM((2, 128, 128), BF16),
            pltpu.VMEM((2, 128, 128), BF16),
            pltpu.VMEM((2, 2, 128, 256), F32),
            pltpu.VMEM((8, 128, 256), F32),
            pltpu.VMEM((8, 128, 256), BF16),
            pltpu.VMEM((2048, 128), F32),
            pltpu.VMEM((2048, 128), F32),
            pltpu.VMEM((2048, 128), F32),
            tiles,
            tiles,
            tiles,
            tiles,
            pltpu.VMEM((128, 512), BF16),
            pltpu.VMEM((512, 128), BF16),
            pltpu.VMEM((512, 512), BF16),
            pltpu.VMEM((512, 512), BF16),
            tiles,
            tiles,
            dma((6,)),
            dma((2,)),
            dma((2,)),
            dma((2, 4)),
            dma((2,)),
        ],
        compiler_params=pltpu.CompilerParams(
            collective_id=0, has_side_effects=True, vmem_limit_bytes=60 << 20
        ),
        name="triangle",
    )(pair, in_gain, proj_weight, gate_weight, out_gain, out_weight)


def solution(mesh):
    in_specs = (P("row", "col", None), P(), P(), P(), P(), P())
    out_specs = (P("row", "col", None), P("row", "col", None))
    return jax.shard_map(local, mesh=mesh, in_specs=in_specs, out_specs=out_specs, check_vma=False)
```

```python
import jax
import jax.numpy as jnp
from jax import lax
from jax.experimental import pallas as pl
from jax.experimental.pallas import tpu as pltpu
from jax.sharding import PartitionSpec as P

EPS = 1e-05
MESH = pl.DeviceIdType.MESH
F32 = jnp.float32
BF16 = jnp.bfloat16
FARTHEST = (-1698185745, 19170134)
PLANES = (2, 1, 3, 0)
TN = (((0,), (0,)), ((), ()))


def norm_rows(values, gain):
    centered = values - jnp.mean(values, axis=0, keepdims=True)
    variance = jnp.mean(centered * centered, axis=0, keepdims=True)
    return (centered * lax.rsqrt(variance + EPS) * gain).astype(BF16)


def sigmoid(values):
    return 0.5 * jnp.tanh(0.5 * values) + 0.5


def swap_halves(first, second):
    return (
        jnp.concatenate([first[:, :64], second[:, :64]], axis=1),
        jnp.concatenate([first[:, 64:], second[:, 64:]], axis=1),
    )


def kernel(
    pair_hbm,
    in_gain_hbm,
    proj_hbm,
    gate_hbm,
    out_gain_hbm,
    outw_hbm,
    out0,
    out1,
    pair,
    proj_w,
    gate_w,
    outw_w,
    in_gain,
    out_gain,
    proj_t,
    gate_t,
    outw_t,
    gains,
    zt,
    normed,
    flat_l,
    flat_r,
    flat_t,
    send_l,
    send_r,
    recv_l,
    recv_r,
    block0,
    block1,
    right,
    right_t,
    tsend,
    trecv,
    load_sem,
    send_sem,
    recv_r_sem,
    recv_l_sem,
    recv_t_sem,
):
    row, col = lax.axis_index("row"), lax.axis_index("col")
    mine = row * 8 + col
    outs = (out0, out1)

    z = row // 4

    def mod4(value):
        return jnp.bitwise_and(value, 3)

    def visit(zs, skip_self, act):
        def both_cores(j, word):
            code = jnp.bitwise_and(lax.shift_right_logical(jnp.int32(word), 4 * j), 15)
            dx, dy = code // 4, mod4(code)
            dx = jnp.bitwise_xor(dx, dx // 2)
            dy = jnp.bitwise_xor(dy, dy // 2)
            tc = jnp.bitwise_xor(col // 4, dx // 2) * 4 + mod4(col + dy)
            tr = zs * 4 + jnp.bitwise_xor(mod4(row), lax.rem(dx, 2) * 2)
            act(jnp.bitwise_xor(tr, 1), tc)
            if skip_self:

                @pl.when(jnp.logical_or(tr != row, tc != col))
                def _():
                    act(tr, tc)

            else:
                act(tr, tc)

        for word in FARTHEST:

            def one(j, carry):
                both_cores(j, word)
                return carry

            lax.fori_loop(0, 8, one, 0, unroll=2)

    barrier = pltpu.get_barrier_semaphore()

    def greet(tr, tc):
        pl.semaphore_signal(barrier, inc=1, device_id=(tr, tc), device_id_type=MESH)

    for dz in PLANES:
        visit(mod4(z + dz), dz == 0, greet)

    loads = [
        pltpu.make_async_copy(src, dst, load_sem.at[i])
        for i, (src, dst) in enumerate(
            (
                (pair_hbm, pair),
                (proj_hbm, proj_w),
                (gate_hbm, gate_w),
                (outw_hbm, outw_w),
                (in_gain_hbm, in_gain),
                (out_gain_hbm, out_gain),
            )
        )
    ]
    for load in loads:
        load.start()
    for load in loads[1:]:
        load.wait()
    for u in range(2):
        for i, gain in enumerate((in_gain, out_gain)):
            flipped = jnp.transpose(jnp.broadcast_to(gain[u : u + 1, :], (128, 128)))
            gains[i, u] = jnp.concatenate([flipped, flipped], axis=1)
        proj_t[u] = jnp.transpose(proj_w[u])
        gate_t[u] = jnp.transpose(gate_w[u])
        outw_t[u] = jnp.transpose(outw_w[u])
    loads[0].wait()

    def project(u, q, side, flat):
        proj = jnp.dot(
            proj_t[u, 256 * side : 256 * side + 256, :], normed[q], preferred_element_type=F32
        )
        gated = sigmoid(proj[:128]) * proj[128:]
        for k in range(2):
            flat[pl.ds(2 * q + k, 128, stride=16), :] = gated[:, 128 * k : 128 * (k + 1)]

    def first(q, carry):
        block = jnp.concatenate(
            [pair[2 * q], pair[2 * q + 16], pair[2 * q + 1], pair[2 * q + 17]], axis=0
        )
        zq = jnp.transpose(block).astype(F32)
        zt[q] = zq
        normed[q] = norm_rows(zq, gains[0, 0])
        project(0, q, 1, flat_r)
        project(0, q, 0, flat_l)
        return carry

    lax.fori_loop(0, 8, first, 0, unroll=4)
    pl.semaphore_wait(barrier, 127)

    def send_side(u, flat, send, recv, sem_of, zs, skip_self):
        def one(tr, tc):
            d = tr * 8 + tc
            send[u, d] = flat[pl.ds(pl.multiple_of(d * 16, 16), 16), :].astype(BF16)
            pltpu.make_async_remote_copy(
                src_ref=send.at[u, d],
                dst_ref=recv.at[u, mine],
                send_sem=send_sem.at[u],
                recv_sem=sem_of,
                device_id=(tr, tc),
                device_id_type=MESH,
            ).start()

        visit(zs, skip_self, one)

    def wait_tiles(ref, sem, count):
        pltpu.make_async_copy(ref.at[pl.ds(0, count)], ref.at[pl.ds(0, count)], sem).wait()

    def own(u, flat, recv):
        recv[u, mine] = flat[pl.ds(pl.multiple_of(mine * 16, 16), 16), :].astype(BF16)

    for u in range(2):
        for dz in PLANES:
            send_side(u, flat_r, send_r, recv_r, recv_r_sem.at[u], mod4(z + dz), dz == 0)
        own(u, flat_r, recv_r)
        if u == 1:

            def late_left(q, carry):
                project(1, q, 0, flat_l)
                return carry

            lax.fori_loop(0, 8, late_left, 0, unroll=4)
        for g, dz in enumerate(PLANES):
            zs = mod4((z if u == 0 else col // 2) + dz)
            send_side(u, flat_l, send_l, recv_l, recv_l_sem.at[u, g], zs, u == 1 or dz == 0)
        own(u, flat_l, recv_l)
        if u == 1:

            def write_first(q, carry):
                flipped = jnp.transpose(zt[q].astype(BF16))
                for k in range(2):
                    out0[2 * q + k] = flipped[128 * k : 128 * k + 64]
                    out0[2 * q + k + 16] = flipped[128 * k + 64 : 128 * k + 128]
                return carry

            lax.fori_loop(0, 8, write_first, 0, unroll=2)

        wait_tiles(recv_r.at[u], recv_r_sem.at[u], 127)

        def arrange(r, carry):
            at = pl.multiple_of(r * 32, 32)
            for m in range(4):
                lo, hi = swap_halves(recv_r[u, r * 8 + 2 * m], recv_r[u, r * 8 + 2 * m + 1])
                right[pl.ds(at, 16), 128 * m : 128 * (m + 1)] = lo
                right[pl.ds(at + 16, 16), 128 * m : 128 * (m + 1)] = hi
            return carry

        lax.fori_loop(0, 16, arrange, 0, unroll=4)
        if u == 0:
            right_t[...] = jnp.transpose(right[...])

        for g, dz in enumerate(PLANES):
            part = mod4(z + (4 - dz))
            if u == 0:
                wait_tiles(recv_l.at[u], recv_l_sem.at[u, g], 31 if dz == 0 else 32)
            else:
                mixed = part == col // 2

                @pl.when(mixed)
                def _():
                    wait_tiles(recv_l.at[u], recv_l_sem.at[u, g], 31)

                @pl.when(jnp.logical_not(mixed))
                def _():
                    wait_tiles(recv_l.at[u], recv_l_sem.at[u, g], 32)

            if u == 0:
                for rr in range(4):
                    for m in range(4):
                        at = (part * 4 + rr) * 8 + 2 * m
                        lo, hi = swap_halves(recv_l[u, at], recv_l[u, at + 1])
                        block0[32 * rr : 32 * rr + 16, 128 * m : 128 * (m + 1)] = lo
                        block0[32 * rr + 16 : 32 * rr + 32, 128 * m : 128 * (m + 1)] = hi
                tri = jnp.dot(block0[...], right_t[...], preferred_element_type=F32).astype(BF16)
            else:
                for r in range(16):
                    at = r * 8 + 2 * part
                    lo, hi = swap_halves(recv_l[u, at], recv_l[u, at + 1])
                    block1[32 * r : 32 * r + 16, :] = lo
                    block1[32 * r + 16 : 32 * r + 32, :] = hi
                tri = lax.dot_general(
                    block1[...], right[...], TN, preferred_element_type=F32
                ).astype(BF16)
            for rr in range(4):
                for m in range(4):
                    lo, hi = swap_halves(
                        tri[32 * rr : 32 * rr + 16, 128 * m : 128 * (m + 1)],
                        tri[32 * rr + 16 : 32 * rr + 32, 128 * m : 128 * (m + 1)],
                    )
                    tsend[u, (part * 4 + rr) * 8 + 2 * m] = lo
                    tsend[u, (part * 4 + rr) * 8 + 2 * m + 1] = hi

            def home(tr, tc):
                pltpu.make_async_remote_copy(
                    src_ref=tsend.at[u, tr * 8 + tc],
                    dst_ref=trecv.at[u, mine],
                    send_sem=send_sem.at[u],
                    recv_sem=recv_t_sem.at[u],
                    device_id=(tr, tc),
                    device_id_type=MESH,
                ).start()

            visit(part, dz == 0, home)
        trecv[u, mine] = tsend[u, mine]
        wait_tiles(trecv.at[u], recv_t_sem.at[u], 127)

        def widen(h, carry):
            flat_t[pl.ds(pl.multiple_of(h * 64, 64), 64), :] = (
                trecv[u, pl.ds(h * 4, 4)].astype(F32).reshape(64, 128)
            )
            return carry

        lax.fori_loop(0, 32, widen, 0, unroll=4)

        def finish(q, carry):
            tri_q = jnp.concatenate(
                [flat_t[pl.ds(2 * q + k, 128, stride=16), :] for k in range(2)], axis=1
            )
            tn = norm_rows(tri_q, gains[1, u])
            gate = sigmoid(jnp.dot(gate_t[u], normed[q], preferred_element_type=F32))
            change = gate * jnp.dot(outw_t[u], tn, preferred_element_type=F32)
            new = (zt[q] + change).astype(BF16)
            if u == 0:
                zq = new.astype(F32)
                zt[q] = zq
                normed[q] = norm_rows(zq, gains[0, 1])
                project(1, q, 1, flat_r)
            else:
                flipped = jnp.transpose(new)
                for k in range(2):
                    out1[2 * q + k] = flipped[128 * k : 128 * k + 64]
                    out1[2 * q + k + 16] = flipped[128 * k + 64 : 128 * k + 128]
            return carry

        lax.fori_loop(0, 8, finish, 0, unroll=4)

    for u in range(2):
        for _ in range(3):
            wait_tiles(send_r.at[u], send_sem.at[u], 127)


def local(pair, in_gain, proj_weight, gate_weight, out_gain, out_weight):
    vmem = pl.BlockSpec(memory_space=pltpu.VMEM)
    hbm = pl.BlockSpec(memory_space=pltpu.HBM)
    shape = jax.ShapeDtypeStruct(pair.shape, BF16)
    tiles = pltpu.VMEM((2, 128, 16, 128), BF16)
    dma = pltpu.SemaphoreType.DMA
    return pl.pallas_call(
        kernel,
        out_shape=(shape, shape),
        in_specs=[hbm] * 6,
        out_specs=(vmem, vmem),
        scratch_shapes=[
            pltpu.VMEM((32, 64, 128), BF16),
            pltpu.VMEM((2, 128, 512), BF16),
            pltpu.VMEM((2, 128, 128), BF16),
            pltpu.VMEM((2, 128, 128), BF16),
            pltpu.VMEM((2, 128), F32),
            pltpu.VMEM((2, 128), F32),
            pltpu.VMEM((2, 512, 128), BF16),
            pltpu.VMEM((2, 128, 128), BF16),
            pltpu.VMEM((2, 128, 128), BF16),
            pltpu.VMEM((2, 2, 128, 256), F32),
            pltpu.VMEM((8, 128, 256), F32),
            pltpu.VMEM((8, 128, 256), BF16),
            pltpu.VMEM((2048, 128), F32),
            pltpu.VMEM((2048, 128), F32),
            pltpu.VMEM((2048, 128), F32),
            tiles,
            tiles,
            tiles,
            tiles,
            pltpu.VMEM((128, 512), BF16),
            pltpu.VMEM((512, 128), BF16),
            pltpu.VMEM((512, 512), BF16),
            pltpu.VMEM((512, 512), BF16),
            tiles,
            tiles,
            dma((6,)),
            dma((2,)),
            dma((2,)),
            dma((2, 4)),
            dma((2,)),
        ],
        compiler_params=pltpu.CompilerParams(
            collective_id=0, has_side_effects=True, vmem_limit_bytes=60 << 20
        ),
        name="triangle",
    )(pair, in_gain, proj_weight, gate_weight, out_gain, out_weight)


def solution(mesh):
    in_specs = (P("row", "col", None), P(), P(), P(), P(), P())
    out_specs = (P("row", "col", None), P("row", "col", None))
    return jax.shard_map(local, mesh=mesh, in_specs=in_specs, out_specs=out_specs, check_vma=False)
```

```python
import jax
import jax.numpy as jnp
from jax import lax
from jax.experimental import pallas as pl
from jax.experimental.pallas import tpu as pltpu
from jax.sharding import PartitionSpec as P

EPS = 1e-05
MESH = pl.DeviceIdType.MESH
F32 = jnp.float32
BF16 = jnp.bfloat16
FARTHEST = 0x3124756
GROUPS = (((2, 1), (2, 0)), ((1, 1), (3, 0)), ((3, 1), (1, 0)), ((0, 1), (0, 0)))
NT = (((1,), (1,)), ((), ()))
TN = (((0,), (0,)), ((), ()))


def norm_rows(values, gain):
    centered = values - jnp.mean(values, axis=0, keepdims=True)
    variance = jnp.mean(centered * centered, axis=0, keepdims=True)
    return (centered * lax.rsqrt(variance + EPS) * gain).astype(BF16)


def sigmoid(values):
    return 0.5 * jnp.tanh(0.5 * values) + 0.5


def swap_halves(first, second):
    return (
        jnp.concatenate([first[:, :64], second[:, :64]], axis=1),
        jnp.concatenate([first[:, 64:], second[:, 64:]], axis=1),
    )


def updated(q, flat_t, zt, normed, gain, gate_weight, out_weight):
    tri_q = jnp.concatenate([flat_t[pl.ds(2 * q + k, 128, stride=16), :] for k in range(2)], axis=1)
    tn = norm_rows(tri_q, gain)
    gate = sigmoid(jnp.dot(gate_weight, normed[q], preferred_element_type=F32))
    change = gate * jnp.dot(out_weight, tn, preferred_element_type=F32)
    return (zt[q] + change).astype(BF16)


def last_kernel(
    first, zt, normed, flat_t, gate_t, outw_t, gain, out0, out1, second, first_sem, second_sem
):
    whole = pltpu.make_async_copy(first, out0, first_sem)
    whole.start()

    def part(q, k):
        rows = pl.ds(2 * q + 16 * k, 2)
        return pltpu.make_async_copy(second.at[rows], out1.at[rows], second_sem)

    def finish(q, carry):
        flipped = jnp.transpose(updated(q, flat_t, zt, normed, gain[...], gate_t[...], outw_t[...]))
        for k in range(2):
            second[2 * q + k] = flipped[128 * k : 128 * k + 64]
            second[2 * q + k + 16] = flipped[128 * k + 64 : 128 * k + 128]
        for k in range(2):
            part(q, k).start()
        return carry

    lax.fori_loop(0, 8, finish, 0, unroll=4)
    pltpu.make_async_copy(second, out1, second_sem).wait()
    whole.wait()


def kernel(
    pair_hbm,
    in_gain_hbm,
    proj_hbm,
    gate_hbm,
    out_gain_hbm,
    outw_hbm,
    out0,
    zt,
    normed,
    flat_t,
    gate_t1,
    outw_t1,
    gain1,
    pair,
    proj_w,
    gate_w,
    outw_w,
    in_gain,
    out_gain,
    proj_t,
    gate_t,
    outw_t,
    gains,
    flat_l,
    flat_r,
    send_l,
    send_r,
    recv_l,
    recv_r,
    block0,
    block1,
    right,
    tsend,
    trecv,
    load_sem,
    send_sem,
    recv_r_sem,
    recv_l_sem,
    recv_t_sem,
):
    row, col = lax.axis_index("row"), lax.axis_index("col")
    mine = row * 8 + col

    z = row // 4

    def mod4(value):
        return jnp.bitwise_and(value, 3)

    def visit(group, act):
        def step(j, carry):
            code = jnp.bitwise_and(lax.shift_right_logical(jnp.int32(FARTHEST), 4 * j), 7)
            tc = jnp.bitwise_xor(col // 4, code // 4) * 4 + mod4(col + code)
            for zs, lo in group:
                for e in range(2):
                    tr = zs * 4 + lo * 2 + jnp.bitwise_xor(jnp.bitwise_and(row, 1), 1 - e)

                    @pl.when(jnp.logical_or(tr != row, tc != col))
                    def _():
                        act(tr, tc)

            return carry

        lax.fori_loop(0, 8, step, 0, unroll=2)

    def shifted(zs, lo, g):
        return [(mod4(zs + dz), jnp.bitwise_xor(lo, dl)) for dz, dl in GROUPS[g]]

    x_lo = lax.rem(row // 2, 2)

    barrier = pltpu.get_barrier_semaphore()

    def greet(tr, tc):
        pl.semaphore_signal(barrier, inc=1, device_id=(tr, tc), device_id_type=MESH)

    for g in range(4):
        visit(shifted(z, x_lo, g), greet)

    loads = [
        pltpu.make_async_copy(src, dst, load_sem.at[i])
        for i, (src, dst) in enumerate(
            (
                (pair_hbm, pair),
                (proj_hbm, proj_w),
                (gate_hbm, gate_w),
                (outw_hbm, outw_w),
                (in_gain_hbm, in_gain),
                (out_gain_hbm, out_gain),
            )
        )
    ]
    for load in loads:
        load.start()
    for load in loads[1:]:
        load.wait()
    for u in range(2):
        for i, gain in enumerate((in_gain, out_gain)):
            flipped = jnp.transpose(jnp.broadcast_to(gain[u : u + 1, :], (128, 128)))
            gains[i, u] = jnp.concatenate([flipped, flipped], axis=1)
        proj_t[u] = jnp.transpose(proj_w[u])
        gate_t[u] = jnp.transpose(gate_w[u])
        outw_t[u] = jnp.transpose(outw_w[u])
    gate_t1[...] = gate_t[1]
    outw_t1[...] = outw_t[1]
    gain1[...] = gains[1, 1]
    loads[0].wait()

    def project(u, q, side, flat):
        proj = jnp.dot(
            proj_t[u, 256 * side : 256 * side + 256, :], normed[q], preferred_element_type=F32
        )
        gated = sigmoid(proj[:128]) * proj[128:]
        for k in range(2):
            flat[pl.ds(2 * q + k, 128, stride=16), :] = gated[:, 128 * k : 128 * (k + 1)]

    def first(q, carry):
        block = jnp.concatenate(
            [pair[2 * q], pair[2 * q + 16], pair[2 * q + 1], pair[2 * q + 17]], axis=0
        )
        zq = jnp.transpose(block).astype(F32)
        zt[q] = zq
        normed[q] = norm_rows(zq, gains[0, 0])
        project(0, q, 1, flat_r)
        project(0, q, 0, flat_l)
        return carry

    lax.fori_loop(0, 8, first, 0, unroll=4)
    pl.semaphore_wait(barrier, 127)

    def send_side(u, flat, send, recv, sem_of, group):
        def one(tr, tc):
            d = tr * 8 + tc
            send[u, d] = flat[pl.ds(pl.multiple_of(d * 16, 16), 16), :].astype(BF16)
            pltpu.make_async_remote_copy(
                src_ref=send.at[u, d],
                dst_ref=recv.at[u, mine],
                send_sem=send_sem.at[u],
                recv_sem=sem_of,
                device_id=(tr, tc),
                device_id_type=MESH,
            ).start()

        visit(group, one)

    def wait_tiles(ref, sem, count):
        pltpu.make_async_copy(ref.at[pl.ds(0, count)], ref.at[pl.ds(0, count)], sem).wait()

    def own(u, flat, recv):
        recv[u, mine] = flat[pl.ds(pl.multiple_of(mine * 16, 16), 16), :].astype(BF16)

    for u in range(2):
        for g in range(4):
            send_side(u, flat_r, send_r, recv_r, recv_r_sem.at[u], shifted(z, x_lo, g))
        own(u, flat_r, recv_r)
        if u == 1:

            def late_left(q, carry):
                project(1, q, 0, flat_l)
                return carry

            lax.fori_loop(0, 8, late_left, 0, unroll=4)
        for g in range(4):
            base = (z, x_lo) if u == 0 else (col // 2, lax.rem(col, 2))
            send_side(u, flat_l, send_l, recv_l, recv_l_sem.at[u, g], shifted(*base, g))
        own(u, flat_l, recv_l)
        if u == 1:

            def write_first(q, carry):
                flipped = jnp.transpose(zt[q].astype(BF16))
                for k in range(2):
                    out0[2 * q + k] = flipped[128 * k : 128 * k + 64]
                    out0[2 * q + k + 16] = flipped[128 * k + 64 : 128 * k + 128]
                return carry

            lax.fori_loop(0, 8, write_first, 0, unroll=2)

        wait_tiles(recv_r.at[u], recv_r_sem.at[u], 127)

        def arrange(r, carry):
            at = pl.multiple_of(r * 32, 32)
            for m in range(4):
                lo, hi = swap_halves(recv_r[u, r * 8 + 2 * m], recv_r[u, r * 8 + 2 * m + 1])
                right[pl.ds(at, 16), 128 * m : 128 * (m + 1)] = lo
                right[pl.ds(at + 16, 16), 128 * m : 128 * (m + 1)] = hi
            return carry

        lax.fori_loop(0, 16, arrange, 0, unroll=4)

        for g in range(4):
            group = [(mod4(z + 4 - dz), jnp.bitwise_xor(x_lo, dl)) for dz, dl in GROUPS[g]]
            rho = [zs * 2 + lo for zs, lo in group]
            if u == 0:
                wait_tiles(recv_l.at[u], recv_l_sem.at[u, g], 31 if (0, 0) in GROUPS[g] else 32)
                for rr in range(4):
                    for m in range(4):
                        at = (rho[rr // 2] * 2 + rr % 2) * 8 + 2 * m
                        lo, hi = swap_halves(recv_l[u, at], recv_l[u, at + 1])
                        block0[32 * rr : 32 * rr + 16, 128 * m : 128 * (m + 1)] = lo
                        block0[32 * rr + 16 : 32 * rr + 32, 128 * m : 128 * (m + 1)] = hi
                tri = lax.dot_general(
                    block0[...], right[...], NT, preferred_element_type=F32
                ).astype(BF16)
            else:
                with_own = jnp.logical_or(rho[0] == col, rho[1] == col)

                @pl.when(with_own)
                def _():
                    wait_tiles(recv_l.at[u], recv_l_sem.at[u, g], 31)

                @pl.when(jnp.logical_not(with_own))
                def _():
                    wait_tiles(recv_l.at[u], recv_l_sem.at[u, g], 32)

                for r in range(16):
                    lo, hi = swap_halves(recv_l[u, r * 8 + rho[0]], recv_l[u, r * 8 + rho[1]])
                    block1[32 * r : 32 * r + 16, :] = lo
                    block1[32 * r + 16 : 32 * r + 32, :] = hi
                tri = lax.dot_general(
                    block1[...], right[...], TN, preferred_element_type=F32
                ).astype(BF16)
            for rr in range(4):
                for m in range(4):
                    lo, hi = swap_halves(
                        tri[32 * rr : 32 * rr + 16, 128 * m : 128 * (m + 1)],
                        tri[32 * rr + 16 : 32 * rr + 32, 128 * m : 128 * (m + 1)],
                    )
                    at = (rho[rr // 2] * 2 + rr % 2) * 8 + 2 * m
                    tsend[u, at] = lo
                    tsend[u, at + 1] = hi

            def home(tr, tc):
                pltpu.make_async_remote_copy(
                    src_ref=tsend.at[u, tr * 8 + tc],
                    dst_ref=trecv.at[u, mine],
                    send_sem=send_sem.at[u],
                    recv_sem=recv_t_sem.at[u],
                    device_id=(tr, tc),
                    device_id_type=MESH,
                ).start()

            visit(group, home)
        trecv[u, mine] = tsend[u, mine]
        wait_tiles(trecv.at[u], recv_t_sem.at[u], 127)

        def widen(h, carry):
            flat_t[pl.ds(pl.multiple_of(h * 64, 64), 64), :] = (
                trecv[u, pl.ds(h * 4, 4)].astype(F32).reshape(64, 128)
            )
            return carry

        lax.fori_loop(0, 32, widen, 0, unroll=4)

        if u == 0:

            def finish(q, carry):
                new = updated(q, flat_t, zt, normed, gains[1, 0], gate_t[0], outw_t[0])
                zq = new.astype(F32)
                zt[q] = zq
                normed[q] = norm_rows(zq, gains[0, 1])
                project(1, q, 1, flat_r)
                return carry

            lax.fori_loop(0, 8, finish, 0, unroll=4)

    for u in range(2):
        for _ in range(3):
            wait_tiles(send_r.at[u], send_sem.at[u], 127)


def local(pair, in_gain, proj_weight, gate_weight, out_gain, out_weight):
    vmem = pl.BlockSpec(memory_space=pltpu.VMEM)
    hbm = pl.BlockSpec(memory_space=pltpu.HBM)
    shape = jax.ShapeDtypeStruct(pair.shape, BF16)
    tiles = pltpu.VMEM((2, 128, 16, 128), BF16)
    dma = pltpu.SemaphoreType.DMA
    operands = [
        pltpu.with_memory_space_constraint(x, pltpu.HBM)
        for x in (pair, in_gain, proj_weight, gate_weight, out_gain, out_weight)
    ]
    handed = pl.pallas_call(
        kernel,
        out_shape=(
            shape,
            jax.ShapeDtypeStruct((8, 128, 256), F32),
            jax.ShapeDtypeStruct((8, 128, 256), BF16),
            jax.ShapeDtypeStruct((2048, 128), F32),
            jax.ShapeDtypeStruct((128, 128), BF16),
            jax.ShapeDtypeStruct((128, 128), BF16),
            jax.ShapeDtypeStruct((128, 256), F32),
        ),
        in_specs=[hbm] * 6,
        out_specs=(vmem,) * 7,
        scratch_shapes=[
            pltpu.VMEM((32, 64, 128), BF16),
            pltpu.VMEM((2, 128, 512), BF16),
            pltpu.VMEM((2, 128, 128), BF16),
            pltpu.VMEM((2, 128, 128), BF16),
            pltpu.VMEM((2, 128), F32),
            pltpu.VMEM((2, 128), F32),
            pltpu.VMEM((2, 512, 128), BF16),
            pltpu.VMEM((2, 128, 128), BF16),
            pltpu.VMEM((2, 128, 128), BF16),
            pltpu.VMEM((2, 2, 128, 256), F32),
            pltpu.VMEM((2048, 128), F32),
            pltpu.VMEM((2048, 128), F32),
            tiles,
            tiles,
            tiles,
            tiles,
            pltpu.VMEM((128, 512), BF16),
            pltpu.VMEM((512, 128), BF16),
            pltpu.VMEM((512, 512), BF16),
            tiles,
            tiles,
            dma((6,)),
            dma((2,)),
            dma((2,)),
            dma((2, 4)),
            dma((2,)),
        ],
        compiler_params=pltpu.CompilerParams(
            collective_id=0, has_side_effects=True, vmem_limit_bytes=24 << 20
        ),
        name="triangle",
    )(*operands)
    return pl.pallas_call(
        last_kernel,
        out_shape=(shape, shape),
        in_specs=[vmem] * 7,
        out_specs=(hbm, hbm),
        scratch_shapes=[pltpu.VMEM((32, 64, 128), BF16), dma, dma],
        compiler_params=pltpu.CompilerParams(vmem_limit_bytes=16 << 20),
        name="last",
    )(*handed)


def solution(mesh):
    in_specs = (P("row", "col", None), P(), P(), P(), P(), P())
    out_specs = (P("row", "col", None), P("row", "col", None))
    return jax.shard_map(local, mesh=mesh, in_specs=in_specs, out_specs=out_specs, check_vma=False)
```

```python
import jax
import jax.numpy as jnp
from jax import lax
from jax.experimental import pallas as pl
from jax.experimental.pallas import tpu as pltpu
from jax.sharding import PartitionSpec as P

EPS = 1e-05
MESH = pl.DeviceIdType.MESH
F32 = jnp.float32
BF16 = jnp.bfloat16
UNROLL = 8
FARTHEST = 0x3124756
GROUPS = (((2, 1), (2, 0)), ((1, 1), (3, 0)), ((3, 1), (1, 0)), ((0, 1), (0, 0)))
NT = (((1,), (1,)), ((), ()))
TN = (((0,), (0,)), ((), ()))


def norm_rows(values, gain):
    centered = values - jnp.mean(values, axis=0, keepdims=True)
    variance = jnp.mean(centered * centered, axis=0, keepdims=True)
    return (centered * lax.rsqrt(variance + EPS) * gain).astype(BF16)


def sigmoid(values):
    return 0.5 * jnp.tanh(0.5 * values) + 0.5


def swap_halves(first, second):
    return (
        jnp.concatenate([first[:, :64], second[:, :64]], axis=1),
        jnp.concatenate([first[:, 64:], second[:, 64:]], axis=1),
    )


def updated(q, flat_t, zt, gate, gain, out_weight):
    tri_q = jnp.concatenate([flat_t[pl.ds(2 * q + k, 128, stride=16), :] for k in range(2)], axis=1)
    tn = norm_rows(tri_q, gain)
    change = gate[q] * jnp.dot(out_weight, tn, preferred_element_type=F32)
    return (zt[q] + change).astype(BF16)


def last_kernel(
    first, zt, gate, flat_t, outw_t, gain, out0, out1, second, first_sem, second_sem
):
    whole = pltpu.make_async_copy(first, out0, first_sem)
    whole.start()

    def part(q, k):
        rows = pl.ds(2 * q + 16 * k, 2)
        return pltpu.make_async_copy(second.at[rows], out1.at[rows], second_sem)

    def finish(q, carry):
        flipped = jnp.transpose(updated(q, flat_t, zt, gate, gain[...], outw_t[...]))
        for k in range(2):
            second[2 * q + k] = flipped[128 * k : 128 * k + 64]
            second[2 * q + k + 16] = flipped[128 * k + 64 : 128 * k + 128]
        for k in range(2):
            part(q, k).start()
        return carry

    lax.fori_loop(0, 8, finish, 0, unroll=4)
    pltpu.make_async_copy(second, out1, second_sem).wait()
    whole.wait()


def kernel(
    pair_hbm,
    in_gain_hbm,
    proj_hbm,
    gate_hbm,
    out_gain_hbm,
    outw_hbm,
    out0,
    zt,
    gate,
    flat_t,
    outw_t1,
    gain1,
    pair,
    proj_w,
    gate_w,
    outw_w,
    in_gain,
    out_gain,
    proj_t,
    gate_t,
    outw_t,
    gains,
    normed,
    flat_l,
    flat_r,
    send_l,
    send_r,
    recv_l,
    recv_r,
    block0,
    block1,
    right,
    tsend,
    trecv,
    load_sem,
    send_r_sem,
    send_l_sem,
    send_t_sem,
    recv_r_sem,
    recv_l_sem,
    recv_t_sem,
):
    row, col = lax.axis_index("row"), lax.axis_index("col")
    mine = row * 8 + col

    z = row // 4

    def mod4(value):
        return jnp.bitwise_and(value, 3)

    def visit(group, skip_self, act, core=None):
        def step(j, carry):
            code = jnp.bitwise_and(lax.shift_right_logical(jnp.int32(FARTHEST), 4 * j), 7)
            tc = jnp.bitwise_xor(col // 4, code // 4) * 4 + mod4(col + code)
            for zs, lo in group:
                for e in range(2) if core is None else (core,):
                    tr = zs * 4 + lo * 2 + e

                    if not skip_self:
                        act(tr, tc)
                    else:

                        @pl.when(jnp.logical_or(tr != row, tc != col))
                        def _():
                            act(tr, tc)

            return carry

        lax.fori_loop(0, 8, step, 0, unroll=UNROLL)

    def shifted(zs, lo, g):
        return [(mod4(zs + dz), jnp.bitwise_xor(lo, dl)) for dz, dl in GROUPS[g]]

    def back(g):
        return [(mod4(z + 4 - dz), jnp.bitwise_xor(x_lo, dl)) for dz, dl in GROUPS[g]]

    def has_own(g):
        return (0, 0) in GROUPS[g]

    x_lo = lax.rem(row // 2, 2)

    loads = [
        pltpu.make_async_copy(src, dst, load_sem.at[i])
        for i, (src, dst) in enumerate(
            (
                (pair_hbm, pair),
                (proj_hbm, proj_w),
                (in_gain_hbm, in_gain),
                (gate_hbm, gate_w),
                (outw_hbm, outw_w),
                (out_gain_hbm, out_gain),
            )
        )
    ]
    for load in loads:
        load.start()
    barrier = pltpu.get_barrier_semaphore()

    def greet(tr, tc):
        pl.semaphore_signal(barrier, inc=1, device_id=(tr, tc), device_id_type=MESH)

    for g in range(4):
        visit(shifted(z, x_lo, g), has_own(g), greet)

    def prepare(u, i, gain):
        flipped = jnp.transpose(jnp.broadcast_to(gain[u : u + 1, :], (128, 128)))
        gains[i, u] = jnp.concatenate([flipped, flipped], axis=1)

    for load in loads[:3]:
        load.wait()
    prepare(0, 0, in_gain)
    proj_t[0] = jnp.transpose(proj_w[0])

    def project(u, q, side, flat):
        proj = jnp.dot(
            proj_t[u, 256 * side : 256 * side + 256, :], normed[q], preferred_element_type=F32
        )
        gated = sigmoid(proj[:128]) * proj[128:]
        for k in range(2):
            flat[pl.ds(2 * q + k, 128, stride=16), :] = gated[:, 128 * k : 128 * (k + 1)]

    def first(q, carry):
        block = jnp.concatenate(
            [pair[2 * q], pair[2 * q + 16], pair[2 * q + 1], pair[2 * q + 17]], axis=0
        )
        zq = jnp.transpose(block).astype(F32)
        zt[q] = zq
        normed[q] = norm_rows(zq, gains[0, 0])
        project(0, q, 1, flat_r)
        return carry

    lax.fori_loop(0, 8, first, 0, unroll=4)
    pl.semaphore_wait(barrier, 127)

    def send_side(u, flat, send, recv, out_sem, in_sem, group, skip_self):
        def one(tr, tc):
            d = tr * 8 + tc
            send[u, d] = flat[pl.ds(pl.multiple_of(d * 16, 16), 16), :].astype(BF16)
            pltpu.make_async_remote_copy(
                src_ref=send.at[u, d],
                dst_ref=recv.at[u, mine],
                send_sem=out_sem,
                recv_sem=in_sem,
                device_id=(tr, tc),
                device_id_type=MESH,
            ).start()

        visit(group, skip_self, one)

    def wait_tiles(ref, sem, count):
        pltpu.make_async_copy(ref.at[pl.ds(0, count)], ref.at[pl.ds(0, count)], sem).wait()

    def own(u, flat, recv):
        recv[u, mine] = flat[pl.ds(pl.multiple_of(mine * 16, 16), 16), :].astype(BF16)

    def wait_left(sem, ref, u, g, group, own_row, static_own):
        if u == 0:
            wait_tiles(ref.at[u], sem.at[u, g], 31 if static_own else 32)
        else:
            rho = [zs * 2 + lo for zs, lo in group]
            with_own = jnp.logical_or(rho[0] == own_row, rho[1] == own_row)

            @pl.when(with_own)
            def _():
                wait_tiles(ref.at[u], sem.at[u, g], 31)

            @pl.when(jnp.logical_not(with_own))
            def _():
                wait_tiles(ref.at[u], sem.at[u, g], 32)

    def left_base(u):
        return (z, x_lo) if u == 0 else (col // 2, lax.rem(col, 2))

    def sent_left(u, g):
        wait_left(send_l_sem, send_l, u, g, shifted(*left_base(u), g), z * 2 + x_lo, has_own(g))

    def sent_right(u):
        wait_tiles(send_r.at[u], send_r_sem.at[u], 127)

    for u in range(2):
        for g in range(4):
            send_side(
                u,
                flat_r,
                send_r,
                recv_r,
                send_r_sem.at[u],
                recv_r_sem.at[u],
                shifted(z, x_lo, g),
                has_own(g),
            )
        own(u, flat_r, recv_r)

        def late_left(q, carry):
            project(u, q, 0, flat_l)
            return carry

        lax.fori_loop(0, 8, late_left, 0, unroll=4)
        for g in range(4):
            send_side(
                u,
                flat_l,
                send_l,
                recv_l,
                send_l_sem.at[u, g],
                recv_l_sem.at[u, g],
                shifted(*left_base(u), g),
                u == 1 or has_own(g),
            )
        own(u, flat_l, recv_l)
        if u == 0:
            for load in loads[3:]:
                load.wait()
            for v in range(2):
                gate_t[v] = jnp.transpose(gate_w[v])
                outw_t[v] = jnp.transpose(outw_w[v])
                prepare(v, 1, out_gain)
            prepare(1, 0, in_gain)
            proj_t[1] = jnp.transpose(proj_w[1])
            outw_t1[...] = outw_t[1]
            gain1[...] = gains[1, 1]

        def open_gate(q, carry):
            gate[q] = sigmoid(jnp.dot(gate_t[u], normed[q], preferred_element_type=F32))
            return carry

        lax.fori_loop(0, 8, open_gate, 0, unroll=4)
        if u == 1:

            def write_first(q, carry):
                flipped = jnp.transpose(zt[q].astype(BF16))
                for k in range(2):
                    out0[2 * q + k] = flipped[128 * k : 128 * k + 64]
                    out0[2 * q + k + 16] = flipped[128 * k + 64 : 128 * k + 128]
                return carry

            lax.fori_loop(0, 8, write_first, 0, unroll=2)

        wait_tiles(recv_r.at[u], recv_r_sem.at[u], 127)

        def arrange(r, carry):
            at = pl.multiple_of(r * 32, 32)
            for m in range(4):
                lo, hi = swap_halves(recv_r[u, r * 8 + 2 * m], recv_r[u, r * 8 + 2 * m + 1])
                right[pl.ds(at, 16), 128 * m : 128 * (m + 1)] = lo
                right[pl.ds(at + 16, 16), 128 * m : 128 * (m + 1)] = hi
            return carry

        lax.fori_loop(0, 16, arrange, 0, unroll=4)

        def home(tr, tc):
            pltpu.make_async_remote_copy(
                src_ref=tsend.at[u, tr * 8 + tc],
                dst_ref=trecv.at[u, mine],
                send_sem=send_t_sem.at[u],
                recv_sem=recv_t_sem.at[u],
                device_id=(tr, tc),
                device_id_type=MESH,
            ).start()

        for g in range(4):
            group = back(g)
            rho = [zs * 2 + lo for zs, lo in group]
            wait_left(recv_l_sem, recv_l, u, g, group, col, has_own(g))
            if u == 0:
                for rr in range(4):
                    for m in range(4):
                        at = (rho[rr // 2] * 2 + rr % 2) * 8 + 2 * m
                        lo, hi = swap_halves(recv_l[u, at], recv_l[u, at + 1])
                        block0[32 * rr : 32 * rr + 16, 128 * m : 128 * (m + 1)] = lo
                        block0[32 * rr + 16 : 32 * rr + 32, 128 * m : 128 * (m + 1)] = hi
                tri = lax.dot_general(
                    block0[...], right[...], NT, preferred_element_type=F32
                ).astype(BF16)
            else:
                for r in range(16):
                    lo, hi = swap_halves(recv_l[u, r * 8 + rho[0]], recv_l[u, r * 8 + rho[1]])
                    block1[32 * r : 32 * r + 16, :] = lo
                    block1[32 * r + 16 : 32 * r + 32, :] = hi
                tri = lax.dot_general(
                    block1[...], right[...], TN, preferred_element_type=F32
                ).astype(BF16)
            for rr in range(4):
                for m in range(4):
                    lo, hi = swap_halves(
                        tri[32 * rr : 32 * rr + 16, 128 * m : 128 * (m + 1)],
                        tri[32 * rr + 16 : 32 * rr + 32, 128 * m : 128 * (m + 1)],
                    )
                    at = (rho[rr // 2] * 2 + rr % 2) * 8 + 2 * m
                    tsend[u, at] = lo
                    tsend[u, at + 1] = hi

            visit(group, has_own(g), home, 0 if u == 0 else None)
        if u == 0:
            for g in range(4):
                visit(back(g), has_own(g), home, 1)
        trecv[u, mine] = tsend[u, mine]
        wait_tiles(trecv.at[u], recv_t_sem.at[u], 127)

        def widen(h, carry):
            flat_t[pl.ds(pl.multiple_of(h * 64, 64), 64), :] = (
                trecv[u, pl.ds(h * 4, 4)].astype(F32).reshape(64, 128)
            )
            return carry

        lax.fori_loop(0, 32, widen, 0, unroll=4)

        if u == 0:

            def finish(q, carry):
                new = updated(q, flat_t, zt, gate, gains[1, 0], outw_t[0])
                zq = new.astype(F32)
                zt[q] = zq
                normed[q] = norm_rows(zq, gains[0, 1])
                project(1, q, 1, flat_r)
                return carry

            lax.fori_loop(0, 8, finish, 0, unroll=4)

    for u in range(2):
        sent_right(u)
        for g in range(4):
            sent_left(u, g)
        wait_tiles(tsend.at[u], send_t_sem.at[u], 127)


def local(pair, in_gain, proj_weight, gate_weight, out_gain, out_weight):
    vmem = pl.BlockSpec(memory_space=pltpu.VMEM)
    hbm = pl.BlockSpec(memory_space=pltpu.HBM)
    shape = jax.ShapeDtypeStruct(pair.shape, BF16)
    tiles = pltpu.VMEM((2, 128, 16, 128), BF16)
    dma = pltpu.SemaphoreType.DMA
    operands = [
        pltpu.with_memory_space_constraint(x, pltpu.HBM)
        for x in (pair, in_gain, proj_weight, gate_weight, out_gain, out_weight)
    ]
    handed = pl.pallas_call(
        kernel,
        out_shape=(
            shape,
            jax.ShapeDtypeStruct((8, 128, 256), F32),
            jax.ShapeDtypeStruct((8, 128, 256), F32),
            jax.ShapeDtypeStruct((2048, 128), F32),
            jax.ShapeDtypeStruct((128, 128), BF16),
            jax.ShapeDtypeStruct((128, 256), F32),
        ),
        in_specs=[hbm] * 6,
        out_specs=(vmem,) * 6,
        scratch_shapes=[
            pltpu.VMEM((32, 64, 128), BF16),
            pltpu.VMEM((2, 128, 512), BF16),
            pltpu.VMEM((2, 128, 128), BF16),
            pltpu.VMEM((2, 128, 128), BF16),
            pltpu.VMEM((2, 128), F32),
            pltpu.VMEM((2, 128), F32),
            pltpu.VMEM((2, 512, 128), BF16),
            pltpu.VMEM((2, 128, 128), BF16),
            pltpu.VMEM((2, 128, 128), BF16),
            pltpu.VMEM((2, 2, 128, 256), F32),
            pltpu.VMEM((8, 128, 256), BF16),
            pltpu.VMEM((2048, 128), F32),
            pltpu.VMEM((2048, 128), F32),
            tiles,
            tiles,
            tiles,
            tiles,
            pltpu.VMEM((128, 512), BF16),
            pltpu.VMEM((512, 128), BF16),
            pltpu.VMEM((512, 512), BF16),
            tiles,
            tiles,
            dma((6,)),
            dma((2,)),
            dma((2, 4)),
            dma((2,)),
            dma((2,)),
            dma((2, 4)),
            dma((2,)),
        ],
        compiler_params=pltpu.CompilerParams(
            collective_id=0, has_side_effects=True, vmem_limit_bytes=24 << 20
        ),
        name="triangle",
    )(*operands)
    return pl.pallas_call(
        last_kernel,
        out_shape=(shape, shape),
        in_specs=[vmem] * 6,
        out_specs=(hbm, hbm),
        scratch_shapes=[pltpu.VMEM((32, 64, 128), BF16), dma, dma],
        compiler_params=pltpu.CompilerParams(vmem_limit_bytes=16 << 20),
        name="last",
    )(*handed)


def solution(mesh):
    in_specs = (P("row", "col", None), P(), P(), P(), P(), P())
    out_specs = (P("row", "col", None), P("row", "col", None))
    return jax.shard_map(local, mesh=mesh, in_specs=in_specs, out_specs=out_specs, check_vma=False)
```

```python
import jax
import jax.numpy as jnp
from jax import lax
from jax.experimental import pallas as pl
from jax.experimental.pallas import tpu as pltpu
from jax.sharding import PartitionSpec as P

EPS = 1e-05
MESH = pl.DeviceIdType.MESH
F32 = jnp.float32
BF16 = jnp.bfloat16
FARTHEST = 0x3124756
GROUPS = (((2, 1), (2, 0)), ((1, 1), (3, 0)), ((3, 1), (1, 0)), ((0, 1), (0, 0)))
NT = (((1,), (1,)), ((), ()))
TN = (((0,), (0,)), ((), ()))


def norm_rows(values, gain):
    centered = values - jnp.mean(values, axis=0, keepdims=True)
    variance = jnp.mean(centered * centered, axis=0, keepdims=True)
    return (centered * lax.rsqrt(variance + EPS) * gain).astype(BF16)


def sigmoid(values):
    return 0.5 * jnp.tanh(0.5 * values) + 0.5


def swap_halves(first, second):
    return (
        jnp.concatenate([first[:, :64], second[:, :64]], axis=1),
        jnp.concatenate([first[:, 64:], second[:, 64:]], axis=1),
    )


def updated(q, flat_t, zt, gate, gain, out_weight):
    tri_q = jnp.concatenate([flat_t[pl.ds(2 * q + k, 128, stride=16), :] for k in range(2)], axis=1)
    tn = norm_rows(tri_q, gain)
    change = gate[q] * jnp.dot(out_weight, tn, preferred_element_type=F32)
    return (zt[q] + change).astype(BF16)


def last_kernel(
    first, zt, gate, flat_t, outw_t, gain, out0, out1, second, first_sem, second_sem
):
    whole = pltpu.make_async_copy(first, out0, first_sem)
    whole.start()

    def part(q, k):
        rows = pl.ds(2 * q + 16 * k, 2)
        return pltpu.make_async_copy(second.at[rows], out1.at[rows], second_sem)

    def finish(q, carry):
        flipped = jnp.transpose(updated(q, flat_t, zt, gate, gain[...], outw_t[...]))
        for k in range(2):
            second[2 * q + k] = flipped[128 * k : 128 * k + 64]
            second[2 * q + k + 16] = flipped[128 * k + 64 : 128 * k + 128]
        for k in range(2):
            part(q, k).start()
        return carry

    lax.fori_loop(0, 8, finish, 0, unroll=4)
    pltpu.make_async_copy(second, out1, second_sem).wait()
    whole.wait()


def kernel(
    pair_hbm,
    in_gain_hbm,
    proj_hbm,
    gate_hbm,
    out_gain_hbm,
    outw_hbm,
    out0,
    zt,
    gate,
    flat_t,
    outw_t1,
    gain1,
    pair,
    proj_w,
    gate_w,
    outw_w,
    in_gain,
    out_gain,
    proj_t,
    gate_t,
    outw_t,
    gains,
    normed,
    flat_l,
    flat_r,
    send_l,
    send_r,
    recv_l,
    recv_r,
    block0,
    block1,
    right,
    tsend,
    trecv,
    load_sem,
    send_r_sem,
    send_l_sem,
    send_t_sem,
    recv_r_sem,
    recv_l_sem,
    recv_t_sem,
):
    row, col = lax.axis_index("row"), lax.axis_index("col")
    mine = row * 8 + col

    z = row // 4

    def mod4(value):
        return jnp.bitwise_and(value, 3)

    def visit(group, skip_self, act, core=None):
        def step(j, carry):
            code = jnp.bitwise_and(lax.shift_right_logical(jnp.int32(FARTHEST), 4 * j), 7)
            tc = jnp.bitwise_xor(col // 4, code // 4) * 4 + mod4(col + code)
            for zs, lo in group:
                for e in range(2) if core is None else (core,):
                    tr = zs * 4 + lo * 2 + e

                    if not skip_self:
                        act(tr, tc)
                    else:

                        @pl.when(jnp.logical_or(tr != row, tc != col))
                        def _():
                            act(tr, tc)

            return carry

        lax.fori_loop(0, 8, step, 0, unroll=8)

    def shifted(zs, lo, g):
        return [(mod4(zs + dz), jnp.bitwise_xor(lo, dl)) for dz, dl in GROUPS[g]]

    def back(g):
        return [(mod4(z + 4 - dz), jnp.bitwise_xor(x_lo, dl)) for dz, dl in GROUPS[g]]

    def has_own(g):
        return (0, 0) in GROUPS[g]

    x_lo = lax.rem(row // 2, 2)

    loads = [
        pltpu.make_async_copy(src, dst, load_sem.at[i])
        for i, (src, dst) in enumerate(
            (
                (pair_hbm, pair),
                (proj_hbm, proj_w),
                (in_gain_hbm, in_gain),
                (gate_hbm, gate_w),
                (outw_hbm, outw_w),
                (out_gain_hbm, out_gain),
            )
        )
    ]
    for load in loads:
        load.start()
    barrier = pltpu.get_barrier_semaphore()

    def greet(tr, tc):
        pl.semaphore_signal(barrier, inc=1, device_id=(tr, tc), device_id_type=MESH)

    for g in range(4):
        visit(shifted(z, x_lo, g), has_own(g), greet)

    def prepare(u, i, gain):
        flipped = jnp.transpose(jnp.broadcast_to(gain[u : u + 1, :], (128, 128)))
        gains[i, u] = jnp.concatenate([flipped, flipped], axis=1)

    for load in loads[:3]:
        load.wait()
    prepare(0, 0, in_gain)
    proj_t[0] = jnp.transpose(proj_w[0])

    def project(u, q, side, flat):
        proj = jnp.dot(
            proj_t[u, 256 * side : 256 * side + 256, :], normed[q], preferred_element_type=F32
        )
        gated = sigmoid(proj[:128]) * proj[128:]
        for k in range(2):
            flat[pl.ds(2 * q + k, 128, stride=16), :] = gated[:, 128 * k : 128 * (k + 1)]

    def first(q, carry):
        block = jnp.concatenate(
            [pair[2 * q], pair[2 * q + 16], pair[2 * q + 1], pair[2 * q + 17]], axis=0
        )
        zq = jnp.transpose(block).astype(F32)
        zt[q] = zq
        normed[q] = norm_rows(zq, gains[0, 0])
        project(0, q, 1, flat_r)
        return carry

    lax.fori_loop(0, 8, first, 0, unroll=4)
    pl.semaphore_wait(barrier, 127)

    def send_side(u, flat, send, recv, out_sem, in_sem, group, skip_self, core):
        def one(tr, tc):
            d = tr * 8 + tc
            send[u, d] = flat[pl.ds(pl.multiple_of(d * 16, 16), 16), :].astype(BF16)
            pltpu.make_async_remote_copy(
                src_ref=send.at[u, d],
                dst_ref=recv.at[u, mine],
                send_sem=out_sem,
                recv_sem=in_sem,
                device_id=(tr, tc),
                device_id_type=MESH,
            ).start()

        visit(group, skip_self, one, core)

    def wait_tiles(ref, sem, count):
        pltpu.make_async_copy(ref.at[pl.ds(0, count)], ref.at[pl.ds(0, count)], sem).wait()

    def own(u, flat, recv):
        recv[u, mine] = flat[pl.ds(pl.multiple_of(mine * 16, 16), 16), :].astype(BF16)

    def wait_left(sem, ref, u, g, group, own_row, static_own):
        if u == 0:
            wait_tiles(ref.at[u], sem.at[u, g], 31 if static_own else 32)
        else:
            rho = [zs * 2 + lo for zs, lo in group]
            with_own = jnp.logical_or(rho[0] == own_row, rho[1] == own_row)

            @pl.when(with_own)
            def _():
                wait_tiles(ref.at[u], sem.at[u, g], 31)

            @pl.when(jnp.logical_not(with_own))
            def _():
                wait_tiles(ref.at[u], sem.at[u, g], 32)

    def left_base(u):
        return (z, x_lo) if u == 0 else (col // 2, lax.rem(col, 2))

    def sent_left(u, g):
        wait_left(send_l_sem, send_l, u, g, shifted(*left_base(u), g), z * 2 + x_lo, has_own(g))

    def sent_right(u):
        wait_tiles(send_r.at[u], send_r_sem.at[u], 127)

    def send_right(u, core):
        for g in range(4):
            send_side(
                u,
                flat_r,
                send_r,
                recv_r,
                send_r_sem.at[u],
                recv_r_sem.at[u],
                shifted(z, x_lo, g),
                has_own(g),
                core,
            )

    def send_left(u, core):
        for g in range(4):
            send_side(
                u,
                flat_l,
                send_l,
                recv_l,
                send_l_sem.at[u, g],
                recv_l_sem.at[u, g],
                shifted(*left_base(u), g),
                u == 1 or has_own(g),
                core,
            )

    for u in range(2):

        def late_left(q, carry):
            project(u, q, 0, flat_l)
            return carry

        send_right(u, 0)
        lax.fori_loop(0, 8, late_left, 0, unroll=4)
        send_left(u, 0)
        send_right(u, 1)
        send_left(u, 1)
        own(u, flat_r, recv_r)
        own(u, flat_l, recv_l)
        if u == 0:
            for load in loads[3:]:
                load.wait()
            for v in range(2):
                gate_t[v] = jnp.transpose(gate_w[v])
                outw_t[v] = jnp.transpose(outw_w[v])
                prepare(v, 1, out_gain)
            prepare(1, 0, in_gain)
            proj_t[1] = jnp.transpose(proj_w[1])
            outw_t1[...] = outw_t[1]
            gain1[...] = gains[1, 1]

        def open_gate(q, carry):
            gate[q] = sigmoid(jnp.dot(gate_t[u], normed[q], preferred_element_type=F32))
            return carry

        lax.fori_loop(0, 8, open_gate, 0, unroll=4)
        if u == 1:

            def write_first(q, carry):
                flipped = jnp.transpose(zt[q].astype(BF16))
                for k in range(2):
                    out0[2 * q + k] = flipped[128 * k : 128 * k + 64]
                    out0[2 * q + k + 16] = flipped[128 * k + 64 : 128 * k + 128]
                return carry

            lax.fori_loop(0, 8, write_first, 0, unroll=2)

        wait_tiles(recv_r.at[u], recv_r_sem.at[u], 127)

        def arrange(r, carry):
            at = pl.multiple_of(r * 32, 32)
            for m in range(4):
                lo, hi = swap_halves(recv_r[u, r * 8 + 2 * m], recv_r[u, r * 8 + 2 * m + 1])
                right[pl.ds(at, 16), 128 * m : 128 * (m + 1)] = lo
                right[pl.ds(at + 16, 16), 128 * m : 128 * (m + 1)] = hi
            return carry

        lax.fori_loop(0, 16, arrange, 0, unroll=4)

        def home(tr, tc):
            pltpu.make_async_remote_copy(
                src_ref=tsend.at[u, tr * 8 + tc],
                dst_ref=trecv.at[u, mine],
                send_sem=send_t_sem.at[u],
                recv_sem=recv_t_sem.at[u],
                device_id=(tr, tc),
                device_id_type=MESH,
            ).start()

        for g in range(4):
            group = back(g)
            rho = [zs * 2 + lo for zs, lo in group]
            wait_left(recv_l_sem, recv_l, u, g, group, col, has_own(g))
            if u == 0:
                for rr in range(4):
                    for m in range(4):
                        at = (rho[rr // 2] * 2 + rr % 2) * 8 + 2 * m
                        lo, hi = swap_halves(recv_l[u, at], recv_l[u, at + 1])
                        block0[32 * rr : 32 * rr + 16, 128 * m : 128 * (m + 1)] = lo
                        block0[32 * rr + 16 : 32 * rr + 32, 128 * m : 128 * (m + 1)] = hi
                tri = lax.dot_general(
                    block0[...], right[...], NT, preferred_element_type=F32
                ).astype(BF16)
            else:
                for r in range(16):
                    lo, hi = swap_halves(recv_l[u, r * 8 + rho[0]], recv_l[u, r * 8 + rho[1]])
                    block1[32 * r : 32 * r + 16, :] = lo
                    block1[32 * r + 16 : 32 * r + 32, :] = hi
                tri = lax.dot_general(
                    block1[...], right[...], TN, preferred_element_type=F32
                ).astype(BF16)
            for rr in range(4):
                for m in range(4):
                    lo, hi = swap_halves(
                        tri[32 * rr : 32 * rr + 16, 128 * m : 128 * (m + 1)],
                        tri[32 * rr + 16 : 32 * rr + 32, 128 * m : 128 * (m + 1)],
                    )
                    at = (rho[rr // 2] * 2 + rr % 2) * 8 + 2 * m
                    tsend[u, at] = lo
                    tsend[u, at + 1] = hi

            visit(group, has_own(g), home)
        trecv[u, mine] = tsend[u, mine]
        wait_tiles(trecv.at[u], recv_t_sem.at[u], 127)

        def widen(h, carry):
            flat_t[pl.ds(pl.multiple_of(h * 64, 64), 64), :] = (
                trecv[u, pl.ds(h * 4, 4)].astype(F32).reshape(64, 128)
            )
            return carry

        lax.fori_loop(0, 32, widen, 0, unroll=4)

        if u == 0:

            def finish(q, carry):
                new = updated(q, flat_t, zt, gate, gains[1, 0], outw_t[0])
                zq = new.astype(F32)
                zt[q] = zq
                normed[q] = norm_rows(zq, gains[0, 1])
                project(1, q, 1, flat_r)
                return carry

            lax.fori_loop(0, 8, finish, 0, unroll=4)

    for u in range(2):
        sent_right(u)
        for g in range(4):
            sent_left(u, g)
        wait_tiles(tsend.at[u], send_t_sem.at[u], 127)


def local(pair, in_gain, proj_weight, gate_weight, out_gain, out_weight):
    vmem = pl.BlockSpec(memory_space=pltpu.VMEM)
    hbm = pl.BlockSpec(memory_space=pltpu.HBM)
    shape = jax.ShapeDtypeStruct(pair.shape, BF16)
    tiles = pltpu.VMEM((2, 128, 16, 128), BF16)
    dma = pltpu.SemaphoreType.DMA
    operands = [
        pltpu.with_memory_space_constraint(x, pltpu.HBM)
        for x in (pair, in_gain, proj_weight, gate_weight, out_gain, out_weight)
    ]
    handed = pl.pallas_call(
        kernel,
        out_shape=(
            shape,
            jax.ShapeDtypeStruct((8, 128, 256), F32),
            jax.ShapeDtypeStruct((8, 128, 256), F32),
            jax.ShapeDtypeStruct((2048, 128), F32),
            jax.ShapeDtypeStruct((128, 128), BF16),
            jax.ShapeDtypeStruct((128, 256), F32),
        ),
        in_specs=[hbm] * 6,
        out_specs=(vmem,) * 6,
        scratch_shapes=[
            pltpu.VMEM((32, 64, 128), BF16),
            pltpu.VMEM((2, 128, 512), BF16),
            pltpu.VMEM((2, 128, 128), BF16),
            pltpu.VMEM((2, 128, 128), BF16),
            pltpu.VMEM((2, 128), F32),
            pltpu.VMEM((2, 128), F32),
            pltpu.VMEM((2, 512, 128), BF16),
            pltpu.VMEM((2, 128, 128), BF16),
            pltpu.VMEM((2, 128, 128), BF16),
            pltpu.VMEM((2, 2, 128, 256), F32),
            pltpu.VMEM((8, 128, 256), BF16),
            pltpu.VMEM((2048, 128), F32),
            pltpu.VMEM((2048, 128), F32),
            tiles,
            tiles,
            tiles,
            tiles,
            pltpu.VMEM((128, 512), BF16),
            pltpu.VMEM((512, 128), BF16),
            pltpu.VMEM((512, 512), BF16),
            tiles,
            tiles,
            dma((6,)),
            dma((2,)),
            dma((2, 4)),
            dma((2,)),
            dma((2,)),
            dma((2, 4)),
            dma((2,)),
        ],
        compiler_params=pltpu.CompilerParams(
            collective_id=0, has_side_effects=True, vmem_limit_bytes=24 << 20
        ),
        name="triangle",
    )(*operands)
    return pl.pallas_call(
        last_kernel,
        out_shape=(shape, shape),
        in_specs=[vmem] * 6,
        out_specs=(hbm, hbm),
        scratch_shapes=[pltpu.VMEM((32, 64, 128), BF16), dma, dma],
        compiler_params=pltpu.CompilerParams(vmem_limit_bytes=16 << 20),
        name="last",
    )(*handed)


def solution(mesh):
    in_specs = (P("row", "col", None), P(), P(), P(), P(), P())
    out_specs = (P("row", "col", None), P("row", "col", None))
    return jax.shard_map(local, mesh=mesh, in_specs=in_specs, out_specs=out_specs, check_vma=False)
```

```python
import jax
import jax.numpy as jnp
from jax import lax
from jax.experimental import pallas as pl
from jax.experimental.pallas import tpu as pltpu
from jax.sharding import PartitionSpec as P

EPS = 1e-05
MESH = pl.DeviceIdType.MESH
F32 = jnp.float32
BF16 = jnp.bfloat16
FARTHEST = 0x3124756
GROUPS = (((2, 1), (2, 0)), ((1, 1), (3, 0)), ((3, 1), (1, 0)), ((0, 1), (0, 0)))
NT = (((1,), (1,)), ((), ()))
TN = (((0,), (0,)), ((), ()))


def norm_rows(values, gain):
    centered = values - jnp.mean(values, axis=0, keepdims=True)
    variance = jnp.mean(centered * centered, axis=0, keepdims=True)
    return (centered * lax.rsqrt(variance + EPS) * gain).astype(BF16)


def sigmoid(values):
    return 0.5 * jnp.tanh(0.5 * values) + 0.5


def swap_halves(first, second):
    return (
        jnp.concatenate([first[:, :64], second[:, :64]], axis=1),
        jnp.concatenate([first[:, 64:], second[:, 64:]], axis=1),
    )


def updated(q, flat_t, zt, gate, gain, out_weight):
    tri_q = jnp.concatenate([flat_t[pl.ds(2 * q + k, 128, stride=16), :] for k in range(2)], axis=1)
    tn = norm_rows(tri_q, gain)
    change = gate[q] * jnp.dot(out_weight, tn, preferred_element_type=F32)
    return (zt[q] + change).astype(BF16)


def last_kernel(
    first, zt, gate, flat_t, outw_t, gain, out0, out1, second, first_sem, second_sem
):
    whole = pltpu.make_async_copy(first, out0, first_sem)
    whole.start()

    def part(q, k):
        rows = pl.ds(2 * q + 16 * k, 2)
        return pltpu.make_async_copy(second.at[rows], out1.at[rows], second_sem)

    def finish(q, carry):
        flipped = jnp.transpose(updated(q, flat_t, zt, gate, gain[...], outw_t[...]))
        for k in range(2):
            second[2 * q + k] = flipped[128 * k : 128 * k + 64]
            second[2 * q + k + 16] = flipped[128 * k + 64 : 128 * k + 128]
        for k in range(2):
            part(q, k).start()
        return carry

    lax.fori_loop(0, 8, finish, 0, unroll=4)
    pltpu.make_async_copy(second, out1, second_sem).wait()
    whole.wait()


def kernel(
    pair_hbm,
    in_gain_hbm,
    proj_hbm,
    gate_hbm,
    out_gain_hbm,
    outw_hbm,
    out0,
    zt,
    gate,
    flat_t,
    outw_t1,
    gain1,
    pair,
    proj_w,
    gate_w,
    outw_w,
    in_gain,
    out_gain,
    proj_t,
    gate_t,
    outw_t,
    gains,
    normed,
    flat_l,
    flat_r,
    send_l,
    send_r,
    recv_l,
    recv_r,
    block0,
    block1,
    right,
    tsend,
    trecv,
    load_sem,
    send_r_sem,
    send_l_sem,
    send_t_sem,
    recv_r_sem,
    recv_l_sem,
    recv_t_sem,
):
    row, col = lax.axis_index("row"), lax.axis_index("col")
    mine = row * 8 + col

    z = row // 4

    def mod4(value):
        return jnp.bitwise_and(value, 3)

    def visit(group, skip_self, act, core=None):
        def step(j, carry):
            code = jnp.bitwise_and(lax.shift_right_logical(jnp.int32(FARTHEST), 4 * j), 7)
            tc = jnp.bitwise_xor(col // 4, code // 4) * 4 + mod4(col + code)
            for zs, lo in group:
                for e in range(2) if core is None else (core,):
                    tr = zs * 4 + lo * 2 + e

                    if not skip_self:
                        act(tr, tc)
                    else:

                        @pl.when(jnp.logical_or(tr != row, tc != col))
                        def _():
                            act(tr, tc)

            return carry

        lax.fori_loop(0, 8, step, 0, unroll=8)

    def shifted(zs, lo, g):
        return [(mod4(zs + dz), jnp.bitwise_xor(lo, dl)) for dz, dl in GROUPS[g]]

    def back(g):
        return [(mod4(z + 4 - dz), jnp.bitwise_xor(x_lo, dl)) for dz, dl in GROUPS[g]]

    def has_own(g):
        return (0, 0) in GROUPS[g]

    x_lo = lax.rem(row // 2, 2)

    loads = [
        pltpu.make_async_copy(src, dst, load_sem.at[i])
        for i, (src, dst) in enumerate(
            (
                (pair_hbm, pair),
                (proj_hbm, proj_w),
                (in_gain_hbm, in_gain),
                (gate_hbm, gate_w),
                (outw_hbm, outw_w),
                (out_gain_hbm, out_gain),
            )
        )
    ]
    for load in loads:
        load.start()
    barrier = pltpu.get_barrier_semaphore()

    def greet(tr, tc):
        pl.semaphore_signal(barrier, inc=1, device_id=(tr, tc), device_id_type=MESH)

    for g in range(4):
        visit(shifted(z, x_lo, g), has_own(g), greet)

    def prepare(u, i, gain):
        flipped = jnp.transpose(jnp.broadcast_to(gain[u : u + 1, :], (128, 128)))
        gains[i, u] = jnp.concatenate([flipped, flipped], axis=1)

    for load in loads[:3]:
        load.wait()
    prepare(0, 0, in_gain)
    proj_t[0] = jnp.transpose(proj_w[0])

    def project(u, q, side, flat):
        proj = jnp.dot(
            proj_t[u, 256 * side : 256 * side + 256, :], normed[q], preferred_element_type=F32
        )
        gated = sigmoid(proj[:128]) * proj[128:]
        for k in range(2):
            flat[pl.ds(2 * q + k, 128, stride=16), :] = gated[:, 128 * k : 128 * (k + 1)]

    def first(q, carry):
        block = jnp.concatenate(
            [pair[2 * q], pair[2 * q + 16], pair[2 * q + 1], pair[2 * q + 17]], axis=0
        )
        zq = jnp.transpose(block).astype(F32)
        zt[q] = zq
        normed[q] = norm_rows(zq, gains[0, 0])
        project(0, q, 1, flat_r)
        return carry

    lax.fori_loop(0, 8, first, 0, unroll=4)
    pl.semaphore_wait(barrier, 127)

    def send_side(u, flat, send, recv, out_sem, in_sem, group, skip_self, core):
        def one(tr, tc):
            d = tr * 8 + tc
            send[u, d] = flat[pl.ds(pl.multiple_of(d * 16, 16), 16), :].astype(BF16)
            pltpu.make_async_remote_copy(
                src_ref=send.at[u, d],
                dst_ref=recv.at[u, mine],
                send_sem=out_sem,
                recv_sem=in_sem,
                device_id=(tr, tc),
                device_id_type=MESH,
            ).start()

        visit(group, skip_self, one, core)

    def wait_tiles(ref, sem, count):
        pltpu.make_async_copy(ref.at[pl.ds(0, count)], ref.at[pl.ds(0, count)], sem).wait()

    def own(u, flat, recv):
        recv[u, mine] = flat[pl.ds(pl.multiple_of(mine * 16, 16), 16), :].astype(BF16)

    def wait_left(sem, ref, u, g, group, own_row, static_own):
        if u == 0:
            wait_tiles(ref.at[u], sem.at[u, g], 31 if static_own else 32)
        else:
            rho = [zs * 2 + lo for zs, lo in group]
            with_own = jnp.logical_or(rho[0] == own_row, rho[1] == own_row)

            @pl.when(with_own)
            def _():
                wait_tiles(ref.at[u], sem.at[u, g], 31)

            @pl.when(jnp.logical_not(with_own))
            def _():
                wait_tiles(ref.at[u], sem.at[u, g], 32)

    def left_base(u):
        return (z, x_lo) if u == 0 else (col // 2, lax.rem(col, 2))

    def sent_left(u, g):
        wait_left(send_l_sem, send_l, u, g, shifted(*left_base(u), g), z * 2 + x_lo, has_own(g))

    def sent_right(u):
        wait_tiles(send_r.at[u], send_r_sem.at[u], 127)

    def send_right(u, core):
        for g in range(4):
            send_side(
                u,
                flat_r,
                send_r,
                recv_r,
                send_r_sem.at[u],
                recv_r_sem.at[u],
                shifted(z, x_lo, g),
                has_own(g),
                core,
            )

    def send_left(u, core):
        for g in range(4):
            send_side(
                u,
                flat_l,
                send_l,
                recv_l,
                send_l_sem.at[u, g],
                recv_l_sem.at[u, g],
                shifted(*left_base(u), g),
                u == 1 or has_own(g),
                core,
            )

    for u in range(2):

        def late_left(q, carry):
            project(u, q, 0, flat_l)
            return carry

        send_right(u, 0)
        lax.fori_loop(0, 8, late_left, 0, unroll=4)
        send_left(u, 0)
        send_right(u, 1)
        send_left(u, 1)
        own(u, flat_r, recv_r)
        own(u, flat_l, recv_l)
        if u == 0:
            for load in loads[3:]:
                load.wait()
            for v in range(2):
                gate_t[v] = jnp.transpose(gate_w[v])
                outw_t[v] = jnp.transpose(outw_w[v])
                prepare(v, 1, out_gain)
            prepare(1, 0, in_gain)
            proj_t[1] = jnp.transpose(proj_w[1])
            outw_t1[...] = outw_t[1]
            gain1[...] = gains[1, 1]

        def open_gate(q, carry):
            gate[q] = sigmoid(jnp.dot(gate_t[u], normed[q], preferred_element_type=F32))
            return carry

        lax.fori_loop(0, 8, open_gate, 0, unroll=4)
        if u == 1:

            def write_first(q, carry):
                flipped = jnp.transpose(zt[q].astype(BF16))
                for k in range(2):
                    out0[2 * q + k] = flipped[128 * k : 128 * k + 64]
                    out0[2 * q + k + 16] = flipped[128 * k + 64 : 128 * k + 128]
                return carry

            lax.fori_loop(0, 8, write_first, 0, unroll=2)

        wait_tiles(recv_r.at[u], recv_r_sem.at[u], 127)

        def arrange(r, carry):
            at = pl.multiple_of(r * 32, 32)
            for m in range(4):
                lo, hi = swap_halves(recv_r[u, r * 8 + 2 * m], recv_r[u, r * 8 + 2 * m + 1])
                right[pl.ds(at, 16), 128 * m : 128 * (m + 1)] = lo
                right[pl.ds(at + 16, 16), 128 * m : 128 * (m + 1)] = hi
            return carry

        lax.fori_loop(0, 16, arrange, 0, unroll=4)

        def home(tr, tc):
            pltpu.make_async_remote_copy(
                src_ref=tsend.at[u, tr * 8 + tc],
                dst_ref=trecv.at[u, mine],
                send_sem=send_t_sem.at[u],
                recv_sem=recv_t_sem.at[u],
                device_id=(tr, tc),
                device_id_type=MESH,
            ).start()

        for g in range(4):
            group = back(g)
            rho = [zs * 2 + lo for zs, lo in group]
            wait_left(recv_l_sem, recv_l, u, g, group, col, has_own(g))
            if u == 0:
                for rr in range(4):
                    for m in range(4):
                        at = (rho[rr // 2] * 2 + rr % 2) * 8 + 2 * m
                        lo, hi = swap_halves(recv_l[u, at], recv_l[u, at + 1])
                        block0[32 * rr : 32 * rr + 16, 128 * m : 128 * (m + 1)] = lo
                        block0[32 * rr + 16 : 32 * rr + 32, 128 * m : 128 * (m + 1)] = hi
                tri = lax.dot_general(
                    block0[...], right[...], NT, preferred_element_type=F32
                ).astype(BF16)
            else:
                for r in range(16):
                    lo, hi = swap_halves(recv_l[u, r * 8 + rho[0]], recv_l[u, r * 8 + rho[1]])
                    block1[32 * r : 32 * r + 16, :] = lo
                    block1[32 * r + 16 : 32 * r + 32, :] = hi
                tri = lax.dot_general(
                    block1[...], right[...], TN, preferred_element_type=F32
                ).astype(BF16)
            for rr in range(4):
                for m in range(4):
                    lo, hi = swap_halves(
                        tri[32 * rr : 32 * rr + 16, 128 * m : 128 * (m + 1)],
                        tri[32 * rr + 16 : 32 * rr + 32, 128 * m : 128 * (m + 1)],
                    )
                    at = (rho[rr // 2] * 2 + rr % 2) * 8 + 2 * m
                    tsend[u, at] = lo
                    tsend[u, at + 1] = hi

            visit(group, has_own(g), home)
        trecv[u, mine] = tsend[u, mine]
        wait_tiles(trecv.at[u], recv_t_sem.at[u], 127)

        def widen(h, carry):
            flat_t[pl.ds(pl.multiple_of(h * 64, 64), 64), :] = (
                trecv[u, pl.ds(h * 4, 4)].astype(F32).reshape(64, 128)
            )
            return carry

        lax.fori_loop(0, 32, widen, 0, unroll=4)

        if u == 0:

            def finish(q, carry):
                new = updated(q, flat_t, zt, gate, gains[1, 0], outw_t[0])
                zq = new.astype(F32)
                zt[q] = zq
                normed[q] = norm_rows(zq, gains[0, 1])
                project(1, q, 1, flat_r)
                return carry

            lax.fori_loop(0, 8, finish, 0, unroll=8)

    for u in range(2):
        sent_right(u)
        for g in range(4):
            sent_left(u, g)
        wait_tiles(tsend.at[u], send_t_sem.at[u], 127)


def local(pair, in_gain, proj_weight, gate_weight, out_gain, out_weight):
    vmem = pl.BlockSpec(memory_space=pltpu.VMEM)
    hbm = pl.BlockSpec(memory_space=pltpu.HBM)
    shape = jax.ShapeDtypeStruct(pair.shape, BF16)
    tiles = pltpu.VMEM((2, 128, 16, 128), BF16)
    dma = pltpu.SemaphoreType.DMA
    operands = [
        pltpu.with_memory_space_constraint(x, pltpu.HBM)
        for x in (pair, in_gain, proj_weight, gate_weight, out_gain, out_weight)
    ]
    handed = pl.pallas_call(
        kernel,
        out_shape=(
            shape,
            jax.ShapeDtypeStruct((8, 128, 256), F32),
            jax.ShapeDtypeStruct((8, 128, 256), F32),
            jax.ShapeDtypeStruct((2048, 128), F32),
            jax.ShapeDtypeStruct((128, 128), BF16),
            jax.ShapeDtypeStruct((128, 256), F32),
        ),
        in_specs=[hbm] * 6,
        out_specs=(vmem,) * 6,
        scratch_shapes=[
            pltpu.VMEM((32, 64, 128), BF16),
            pltpu.VMEM((2, 128, 512), BF16),
            pltpu.VMEM((2, 128, 128), BF16),
            pltpu.VMEM((2, 128, 128), BF16),
            pltpu.VMEM((2, 128), F32),
            pltpu.VMEM((2, 128), F32),
            pltpu.VMEM((2, 512, 128), BF16),
            pltpu.VMEM((2, 128, 128), BF16),
            pltpu.VMEM((2, 128, 128), BF16),
            pltpu.VMEM((2, 2, 128, 256), F32),
            pltpu.VMEM((8, 128, 256), BF16),
            pltpu.VMEM((2048, 128), F32),
            pltpu.VMEM((2048, 128), F32),
            tiles,
            tiles,
            tiles,
            tiles,
            pltpu.VMEM((128, 512), BF16),
            pltpu.VMEM((512, 128), BF16),
            pltpu.VMEM((512, 512), BF16),
            tiles,
            tiles,
            dma((6,)),
            dma((2,)),
            dma((2, 4)),
            dma((2,)),
            dma((2,)),
            dma((2, 4)),
            dma((2,)),
        ],
        compiler_params=pltpu.CompilerParams(
            collective_id=0, has_side_effects=True, vmem_limit_bytes=24 << 20
        ),
        name="triangle",
    )(*operands)
    return pl.pallas_call(
        last_kernel,
        out_shape=(shape, shape),
        in_specs=[vmem] * 6,
        out_specs=(hbm, hbm),
        scratch_shapes=[pltpu.VMEM((32, 64, 128), BF16), dma, dma],
        compiler_params=pltpu.CompilerParams(vmem_limit_bytes=16 << 20),
        name="last",
    )(*handed)


def solution(mesh):
    in_specs = (P("row", "col", None), P(), P(), P(), P(), P())
    out_specs = (P("row", "col", None), P("row", "col", None))
    return jax.shard_map(local, mesh=mesh, in_specs=in_specs, out_specs=out_specs, check_vma=False)
```

```python
import jax
import jax.numpy as jnp
from jax import lax
from jax.experimental import pallas as pl
from jax.experimental.pallas import tpu as pltpu
from jax.sharding import PartitionSpec as P

EPS = 1e-05
FLAT = 128 * 16 + 16
MESH = pl.DeviceIdType.MESH
F32 = jnp.float32
BF16 = jnp.bfloat16
FARTHEST = 0x3124756
GROUPS = (((2, 1), (2, 0)), ((1, 1), (3, 0)), ((3, 1), (1, 0)), ((0, 1), (0, 0)))
NT = (((1,), (1,)), ((), ()))
TN = (((0,), (0,)), ((), ()))


def norm_rows(values, gain):
    centered = values - jnp.mean(values, axis=0, keepdims=True)
    variance = jnp.mean(centered * centered, axis=0, keepdims=True)
    return (centered * lax.rsqrt(variance + EPS) * gain).astype(BF16)


def sigmoid(values):
    return 0.5 * jnp.tanh(0.5 * values) + 0.5


def swap_halves(first, second):
    return (
        jnp.concatenate([first[:, :64], second[:, :64]], axis=1),
        jnp.concatenate([first[:, 64:], second[:, 64:]], axis=1),
    )


def updated(q, flat_t, zt, gate, gain, out_weight):
    tri_q = jnp.concatenate([flat_t[pl.ds(2 * q + k, 128, stride=16), :] for k in range(2)], axis=1)
    tn = norm_rows(tri_q, gain)
    change = gate[q] * jnp.dot(out_weight, tn, preferred_element_type=F32)
    return (zt[q] + change).astype(BF16)


def last_kernel(
    first, zt, gate, flat_t, outw_t, gain, out0, out1, second, first_sem, second_sem
):
    whole = pltpu.make_async_copy(first, out0, first_sem)
    whole.start()

    def part(q, k):
        rows = pl.ds(2 * q + 16 * k, 2)
        return pltpu.make_async_copy(second.at[rows], out1.at[rows], second_sem)

    def finish(q, carry):
        flipped = jnp.transpose(updated(q, flat_t, zt, gate, gain[...], outw_t[...]))
        for k in range(2):
            second[2 * q + k] = flipped[128 * k : 128 * k + 64]
            second[2 * q + k + 16] = flipped[128 * k + 64 : 128 * k + 128]
        for k in range(2):
            part(q, k).start()
        return carry

    lax.fori_loop(0, 8, finish, 0, unroll=4)
    pltpu.make_async_copy(second, out1, second_sem).wait()
    whole.wait()


def kernel(
    pair_hbm,
    in_gain_hbm,
    proj_hbm,
    gate_hbm,
    out_gain_hbm,
    outw_hbm,
    out0,
    zt,
    gate,
    flat_t,
    outw_t1,
    gain1,
    pair,
    proj_w,
    gate_w,
    outw_w,
    in_gain,
    out_gain,
    proj_t,
    gate_t,
    outw_t,
    gains,
    normed,
    flat_l,
    flat_r,
    send_l,
    send_r,
    recv_l,
    recv_r,
    block0,
    block1,
    right,
    tsend,
    trecv,
    load_sem,
    send_r_sem,
    send_l_sem,
    send_t_sem,
    recv_r_sem,
    recv_l_sem,
    recv_t_sem,
):
    row, col = lax.axis_index("row"), lax.axis_index("col")
    mine = row * 8 + col

    z = row // 4

    def mod4(value):
        return jnp.bitwise_and(value, 3)

    def visit(group, skip_self, act, core=None):
        def step(j, carry):
            code = jnp.bitwise_and(lax.shift_right_logical(jnp.int32(FARTHEST), 4 * j), 7)
            tc = jnp.bitwise_xor(col // 4, code // 4) * 4 + mod4(col + code)
            for zs, lo in group:
                for e in range(2) if core is None else (core,):
                    tr = zs * 4 + lo * 2 + e

                    if not skip_self:
                        act(tr, tc)
                    else:

                        @pl.when(jnp.logical_or(tr != row, tc != col))
                        def _():
                            act(tr, tc)

            return carry

        lax.fori_loop(0, 8, step, 0, unroll=8)

    def shifted(zs, lo, g):
        return [(mod4(zs + dz), jnp.bitwise_xor(lo, dl)) for dz, dl in GROUPS[g]]

    def back(g):
        return [(mod4(z + 4 - dz), jnp.bitwise_xor(x_lo, dl)) for dz, dl in GROUPS[g]]

    def has_own(g):
        return (0, 0) in GROUPS[g]

    x_lo = lax.rem(row // 2, 2)

    loads = [
        pltpu.make_async_copy(src, dst, load_sem.at[i])
        for i, (src, dst) in enumerate(
            (
                (pair_hbm, pair),
                (proj_hbm, proj_w),
                (in_gain_hbm, in_gain),
                (gate_hbm, gate_w),
                (outw_hbm, outw_w),
                (out_gain_hbm, out_gain),
            )
        )
    ]
    for load in loads:
        load.start()
    barrier = pltpu.get_barrier_semaphore()

    def greet(tr, tc):
        pl.semaphore_signal(barrier, inc=1, device_id=(tr, tc), device_id_type=MESH)

    for g in range(4):
        visit(shifted(z, x_lo, g), has_own(g), greet)

    def prepare(u, i, gain):
        flipped = jnp.transpose(jnp.broadcast_to(gain[u : u + 1, :], (128, 128)))
        gains[i, u] = jnp.concatenate([flipped, flipped], axis=1)

    for load in loads[:3]:
        load.wait()
    prepare(0, 0, in_gain)
    proj_t[0] = jnp.transpose(proj_w[0])

    def project(u, q, side, flat):
        proj = jnp.dot(
            proj_t[u, 256 * side : 256 * side + 256, :], normed[q], preferred_element_type=F32
        )
        gated = sigmoid(proj[:128]) * proj[128:]
        for k in range(2):
            flat[pl.ds(2 * q + k, 128, stride=16), :] = gated[:, 128 * k : 128 * (k + 1)]

    def first(q, carry):
        block = jnp.concatenate(
            [pair[2 * q], pair[2 * q + 16], pair[2 * q + 1], pair[2 * q + 17]], axis=0
        )
        zq = jnp.transpose(block).astype(F32)
        zt[q] = zq
        normed[q] = norm_rows(zq, gains[0, 0])
        project(0, q, 1, flat_r)
        return carry

    lax.fori_loop(0, 8, first, 0, unroll=4)
    pl.semaphore_wait(barrier, 127)

    def send_side(u, flat, send, recv, out_sem, in_sem, group, skip_self, core):
        def one(tr, tc):
            d = tr * 8 + tc
            send[u, d] = flat[pl.ds(pl.multiple_of(d * 16, 16), 16), :].astype(BF16)
            pltpu.make_async_remote_copy(
                src_ref=send.at[u, d],
                dst_ref=recv.at[u, mine],
                send_sem=out_sem,
                recv_sem=in_sem,
                device_id=(tr, tc),
                device_id_type=MESH,
            ).start()

        visit(group, skip_self, one, core)

    def wait_tiles(ref, sem, count):
        pltpu.make_async_copy(ref.at[pl.ds(0, count)], ref.at[pl.ds(0, count)], sem).wait()

    def own(u, flat, recv):
        recv[u, mine] = flat[pl.ds(pl.multiple_of(mine * 16, 16), 16), :].astype(BF16)

    def wait_left(sem, ref, u, g, group, own_row, static_own):
        if u == 0:
            wait_tiles(ref.at[u], sem.at[u, g], 31 if static_own else 32)
        else:
            rho = [zs * 2 + lo for zs, lo in group]
            with_own = jnp.logical_or(rho[0] == own_row, rho[1] == own_row)

            @pl.when(with_own)
            def _():
                wait_tiles(ref.at[u], sem.at[u, g], 31)

            @pl.when(jnp.logical_not(with_own))
            def _():
                wait_tiles(ref.at[u], sem.at[u, g], 32)

    def left_base(u):
        return (z, x_lo) if u == 0 else (col // 2, lax.rem(col, 2))

    def sent_left(u, g):
        wait_left(send_l_sem, send_l, u, g, shifted(*left_base(u), g), z * 2 + x_lo, has_own(g))

    def sent_right(u):
        wait_tiles(send_r.at[u], send_r_sem.at[u], 127)

    def send_right(u, core):
        for g in range(4):
            send_side(
                u,
                flat_r,
                send_r,
                recv_r,
                send_r_sem.at[u],
                recv_r_sem.at[u],
                shifted(z, x_lo, g),
                has_own(g),
                core,
            )

    def send_left(u, core):
        for g in range(4):
            send_side(
                u,
                flat_l,
                send_l,
                recv_l,
                send_l_sem.at[u, g],
                recv_l_sem.at[u, g],
                shifted(*left_base(u), g),
                u == 1 or has_own(g),
                core,
            )

    for u in range(2):

        def late_left(q, carry):
            project(u, q, 0, flat_l)
            return carry

        send_right(u, 0)
        lax.fori_loop(0, 8, late_left, 0, unroll=4)
        send_left(u, 0)
        send_right(u, 1)
        send_left(u, 1)
        own(u, flat_r, recv_r)
        own(u, flat_l, recv_l)
        if u == 0:
            for load in loads[3:]:
                load.wait()
            for v in range(2):
                gate_t[v] = jnp.transpose(gate_w[v])
                outw_t[v] = jnp.transpose(outw_w[v])
                prepare(v, 1, out_gain)
            prepare(1, 0, in_gain)
            proj_t[1] = jnp.transpose(proj_w[1])
            outw_t1[...] = outw_t[1]
            gain1[...] = gains[1, 1]

        def open_gate(q, carry):
            gate[q] = sigmoid(jnp.dot(gate_t[u], normed[q], preferred_element_type=F32))
            return carry

        lax.fori_loop(0, 8, open_gate, 0, unroll=4)
        if u == 1:

            def write_first(q, carry):
                flipped = jnp.transpose(zt[q].astype(BF16))
                for k in range(2):
                    out0[2 * q + k] = flipped[128 * k : 128 * k + 64]
                    out0[2 * q + k + 16] = flipped[128 * k + 64 : 128 * k + 128]
                return carry

            lax.fori_loop(0, 8, write_first, 0, unroll=2)

        wait_tiles(recv_r.at[u], recv_r_sem.at[u], 127)

        def arrange(r, carry):
            at = pl.multiple_of(r * 32, 32)
            for m in range(4):
                lo, hi = swap_halves(recv_r[u, r * 8 + 2 * m], recv_r[u, r * 8 + 2 * m + 1])
                right[pl.ds(at, 16), 128 * m : 128 * (m + 1)] = lo
                right[pl.ds(at + 16, 16), 128 * m : 128 * (m + 1)] = hi
            return carry

        lax.fori_loop(0, 16, arrange, 0, unroll=4)

        def home(tr, tc):
            pltpu.make_async_remote_copy(
                src_ref=tsend.at[u, tr * 8 + tc],
                dst_ref=trecv.at[u, mine],
                send_sem=send_t_sem.at[u],
                recv_sem=recv_t_sem.at[u],
                device_id=(tr, tc),
                device_id_type=MESH,
            ).start()

        for g in range(4):
            group = back(g)
            rho = [zs * 2 + lo for zs, lo in group]
            wait_left(recv_l_sem, recv_l, u, g, group, col, has_own(g))
            if u == 0:
                for rr in range(4):
                    for m in range(4):
                        at = (rho[rr // 2] * 2 + rr % 2) * 8 + 2 * m
                        lo, hi = swap_halves(recv_l[u, at], recv_l[u, at + 1])
                        block0[32 * rr : 32 * rr + 16, 128 * m : 128 * (m + 1)] = lo
                        block0[32 * rr + 16 : 32 * rr + 32, 128 * m : 128 * (m + 1)] = hi
                tri = lax.dot_general(
                    block0[...], right[...], NT, preferred_element_type=F32
                ).astype(BF16)
            else:
                for r in range(16):
                    lo, hi = swap_halves(recv_l[u, r * 8 + rho[0]], recv_l[u, r * 8 + rho[1]])
                    block1[32 * r : 32 * r + 16, :] = lo
                    block1[32 * r + 16 : 32 * r + 32, :] = hi
                tri = lax.dot_general(
                    block1[...], right[...], TN, preferred_element_type=F32
                ).astype(BF16)
            for rr in range(4):
                for m in range(4):
                    lo, hi = swap_halves(
                        tri[32 * rr : 32 * rr + 16, 128 * m : 128 * (m + 1)],
                        tri[32 * rr + 16 : 32 * rr + 32, 128 * m : 128 * (m + 1)],
                    )
                    at = (rho[rr // 2] * 2 + rr % 2) * 8 + 2 * m
                    tsend[u, at] = lo
                    tsend[u, at + 1] = hi

            visit(group, has_own(g), home)
        trecv[u, mine] = tsend[u, mine]
        wait_tiles(trecv.at[u], recv_t_sem.at[u], 127)

        def widen(h, carry):
            flat_t[pl.ds(pl.multiple_of(h * 64, 64), 64), :] = (
                trecv[u, pl.ds(h * 4, 4)].astype(F32).reshape(64, 128)
            )
            return carry

        lax.fori_loop(0, 32, widen, 0, unroll=4)

        if u == 0:

            def finish(q, carry):
                new = updated(q, flat_t, zt, gate, gains[1, 0], outw_t[0])
                zq = new.astype(F32)
                zt[q] = zq
                normed[q] = norm_rows(zq, gains[0, 1])
                project(1, q, 1, flat_r)
                return carry

            lax.fori_loop(0, 8, finish, 0, unroll=8)

    for u in range(2):
        sent_right(u)
        for g in range(4):
            sent_left(u, g)
        wait_tiles(tsend.at[u], send_t_sem.at[u], 127)


def local(pair, in_gain, proj_weight, gate_weight, out_gain, out_weight):
    vmem = pl.BlockSpec(memory_space=pltpu.VMEM)
    hbm = pl.BlockSpec(memory_space=pltpu.HBM)
    shape = jax.ShapeDtypeStruct(pair.shape, BF16)
    tiles = pltpu.VMEM((2, 128, 16, 128), BF16)
    dma = pltpu.SemaphoreType.DMA
    operands = [
        pltpu.with_memory_space_constraint(x, pltpu.HBM)
        for x in (pair, in_gain, proj_weight, gate_weight, out_gain, out_weight)
    ]
    handed = pl.pallas_call(
        kernel,
        out_shape=(
            shape,
            jax.ShapeDtypeStruct((8, 128, 256), F32),
            jax.ShapeDtypeStruct((8, 128, 256), F32),
            jax.ShapeDtypeStruct((FLAT, 128), F32),
            jax.ShapeDtypeStruct((128, 128), BF16),
            jax.ShapeDtypeStruct((128, 256), F32),
        ),
        in_specs=[hbm] * 6,
        out_specs=(vmem,) * 6,
        scratch_shapes=[
            pltpu.VMEM((32, 64, 128), BF16),
            pltpu.VMEM((2, 128, 512), BF16),
            pltpu.VMEM((2, 128, 128), BF16),
            pltpu.VMEM((2, 128, 128), BF16),
            pltpu.VMEM((2, 128), F32),
            pltpu.VMEM((2, 128), F32),
            pltpu.VMEM((2, 512, 128), BF16),
            pltpu.VMEM((2, 128, 128), BF16),
            pltpu.VMEM((2, 128, 128), BF16),
            pltpu.VMEM((2, 2, 128, 256), F32),
            pltpu.VMEM((8, 128, 256), BF16),
            pltpu.VMEM((FLAT, 128), F32),
            pltpu.VMEM((FLAT, 128), F32),
            tiles,
            tiles,
            tiles,
            tiles,
            pltpu.VMEM((128, 512), BF16),
            pltpu.VMEM((512, 128), BF16),
            pltpu.VMEM((512, 512), BF16),
            tiles,
            tiles,
            dma((6,)),
            dma((2,)),
            dma((2, 4)),
            dma((2,)),
            dma((2,)),
            dma((2, 4)),
            dma((2,)),
        ],
        compiler_params=pltpu.CompilerParams(
            collective_id=0, has_side_effects=True, vmem_limit_bytes=24 << 20
        ),
        name="triangle",
    )(*operands)
    return pl.pallas_call(
        last_kernel,
        out_shape=(shape, shape),
        in_specs=[vmem] * 6,
        out_specs=(hbm, hbm),
        scratch_shapes=[pltpu.VMEM((32, 64, 128), BF16), dma, dma],
        compiler_params=pltpu.CompilerParams(vmem_limit_bytes=16 << 20),
        name="last",
    )(*handed)


def solution(mesh):
    in_specs = (P("row", "col", None), P(), P(), P(), P(), P())
    out_specs = (P("row", "col", None), P("row", "col", None))
    return jax.shard_map(local, mesh=mesh, in_specs=in_specs, out_specs=out_specs, check_vma=False)
```
